1024 devices in a mesh: resp: 4 (over x), ep: 32 (over y, z_lo), kv: 8 (over z_hi, core).
Axes of the slice: x: 4, y: 4, z: 32 (z_hi: 4, z_lo: 8; z = z_hi * 8 + z_lo), core: 2. Of those that a mesh axis runs over, the one named last changes fastest.
Arguments:
- lengths: int32 [4], replicated, may hold values from 1 to 4096, 8192 in all
- queries: bfloat16 [4, 4096, 4096], P('resp', 'ep'), may hold values from -140 to 140
- grad_out: bfloat16 [4, 4096, 4096], P('resp', 'ep'), may hold values from -6 to 6
- prompt_keys: bfloat16 [1024, 256], P(('ep', 'kv')), may hold values from -7 to 7
- prompt_values: bfloat16 [1024, 256], P(('ep', 'kv')), may hold values from -6 to 6
Outputs:
- grad_queries: float32 [4, 4096, 4096], P('resp', 'ep', 'kv')
- grad_keys: float32 [1024, 256], P(('ep', 'kv'))
- grad_values: float32 [1024, 256], P(('ep', 'kv'))
The draws below stay inside these ranges and needn't reach their ends.
Inputs may be any that keep to these rules, and one draw needn't show every extreme that they name: `lengths`: the longest response fills all 4096 slots.
All inputs are finite; a program needn't handle non-finite values.
Results may differ from the reference program's by a relative error of at most 0.0029.
Values may be sent and summed in bfloat16 or wider, within the bound.
A program may use at most 32 MiB of HBM per device.

```python
import math
import jax
import jax.numpy as jnp
import numpy as np
from jax import lax

HQ = 32
KVH = 2
HD = 128
ROWS = 128
RESPONSES = 4
MAXLEN = 4096
PROMPT = 1024
N_RESP = 4
N_EP = 32


def key_table(key):
    return jax.random.normal(jax.random.fold_in(key, 11), (PROMPT, KVH, HD), jnp.float32)


def draw_prompt_keys(key, part):
    table = key_table(key)
    table = jnp.clip(table, -6.5, 6.5)
    return table.reshape(PROMPT, KVH * HD).astype(jnp.bfloat16)


def draw_queries(key, part):
    key = jax.random.fold_in(key, 5)
    fresh = jnp.clip(jax.random.normal(key, (RESPONSES, MAXLEN, HQ, HD), jnp.float32), -6.0, 6.0)
    return fresh.reshape(RESPONSES, MAXLEN, HQ * HD).astype(jnp.bfloat16)


def block_levels(stream_key, dims, shards, least, top_value):
    level, own = 1.0, jax.random.fold_in(stream_key, 6)
    for dim, parts in shards:
        draws = jnp.exp(jax.random.uniform(jax.random.fold_in(own, dim), (parts,), jnp.float32, least / len(shards), top_value / len(shards)))
        level = level * jnp.repeat(draws, dims[dim] // parts).reshape([-1 if axis == dim else 1 for axis in range(len(dims))])
    return level


def length_profile(number_of, total, most, skew):
    portions = [(1 << 20) // math.isqrt(grade ** skew) + 1 for grade in range(2, number_of + 1)]
    surplus, holding = total - most - (number_of - 1), [1] * (number_of - 1)
    while surplus > 0:
        movable = [i for i in range(number_of - 1) if holding[i] < most]
        pool, remaining = sum([portions[i] for i in movable]), surplus
        for i in movable:
            more = min(most - holding[i], max(1, remaining * portions[i] // pool), surplus)
            holding[i] = holding[i] + more
            surplus = surplus - more
    return np.array([most] + holding)


def ragged(key, count, total, limit, lean):
    if count == 2:
        one = jax.random.randint(key, (), max(1, total - limit), min(limit, total - 1) + 1)
        return jnp.stack([one, total - one])
    tallies = jnp.asarray(length_profile(count, total, limit, lean), jnp.int32)
    twos = (count - 1) // 2
    donor, receiver = tallies[1:1 + 2 * twos:2], tallies[2:2 + 2 * twos:2]
    margin = jnp.minimum(donor - 1, limit - receiver)
    passed = jax.random.randint(jax.random.fold_in(key, 1), (twos,), 0, 1 << 20) % (margin + 1)
    tallies = tallies.at[1:1 + 2 * twos:2].set(donor - passed).at[2:2 + 2 * twos:2].set(receiver + passed)
    return tallies[jax.random.permutation(jax.random.fold_in(key, 2), count)]


def centred(key, extent, scale, limit, split=(), held_as=jnp.bfloat16):
    entries = scale * jax.random.normal(key, extent, jnp.float32)
    if split:
        entries = entries * block_levels(key, extent, split, -0.22, 0.18)
    return jnp.clip(entries, -limit, limit).astype(held_as)


def setup_inputs(seed: int = 0) -> dict:
    key_of = jax.random.split(jax.random.key(seed), 6)
    lengths = ragged(key_of[0], RESPONSES, ROWS * N_EP * (N_RESP + 2) // 3, ROWS * N_EP, 1).astype(jnp.int32)
    queries = draw_queries(jax.random.fold_in(key_of[5], 71), 0)
    grad_out = centred(key_of[2], (RESPONSES, MAXLEN, HQ * HD), 1.0, 6.0, ((0, 4), (1, 32)))
    prompt_keys = draw_prompt_keys(jax.random.fold_in(key_of[5], 71), 0)
    prompt_values = centred(key_of[4], (PROMPT, KVH * HD), 1.0, 6.0, ((0, 256),))
    return {"lengths": lengths, "queries": queries, "grad_out": grad_out, "prompt_keys": prompt_keys, "prompt_values": prompt_values}


def reference(lengths, queries, grad_out, prompt_keys, prompt_values):
    groups = HQ // KVH
    score_scale = 1.0 / math.sqrt(HD)
    keys = prompt_keys.reshape(PROMPT, KVH, HD).astype(jnp.float32)
    values = prompt_values.reshape(PROMPT, KVH, HD).astype(jnp.float32)
    block = min(512, MAXLEN)
    count = MAXLEN // block
    positions = jnp.arange(MAXLEN, dtype=jnp.int32)
    valid = positions[None, :] < lengths[:, None]
    masked = jnp.where(valid[:, :, None], grad_out, jnp.zeros((), grad_out.dtype))
    q_blocks = queries.reshape(RESPONSES * count, block, KVH, groups, HD)
    d_blocks = masked.reshape(RESPONSES * count, block, KVH, groups, HD)

    def step(carry, pair):
        q_block, d_block = pair
        q_float = q_block.astype(jnp.float32)
        d_float = d_block.astype(jnp.float32)
        scores = jnp.einsum('bhgd,phd->bhgp', q_float, keys) * score_scale
        top = lax.optimization_barrier(jnp.max(scores, axis=-1, keepdims=True))
        expo = jnp.exp(scores - top)
        prob = expo / lax.optimization_barrier(jnp.sum(expo, axis=-1, keepdims=True))
        dprob = jnp.einsum('bhgd,phd->bhgp', d_float, values)
        delta = lax.optimization_barrier(jnp.sum(prob * dprob, axis=-1, keepdims=True))
        dscore = lax.optimization_barrier((prob * (dprob - delta)).astype(jnp.bfloat16)).astype(jnp.float32)
        prob_low = lax.optimization_barrier(prob.astype(jnp.bfloat16)).astype(jnp.float32)
        grad_q = jnp.einsum('bhgp,phd->bhgd', dscore, keys) * score_scale
        grad_k = carry[0] + jnp.einsum('bhgp,bhgd->phd', dscore, q_float) * score_scale
        grad_v = carry[1] + jnp.einsum('bhgp,bhgd->phd', prob_low, d_float)
        return ((grad_k, grad_v), grad_q)
    zeros = jnp.zeros((PROMPT, KVH, HD), jnp.float32)
    (grad_k, grad_v), grad_q = lax.scan(step, (zeros, zeros), (q_blocks, d_blocks))
    return (grad_q.reshape(RESPONSES, MAXLEN, HQ * HD), grad_k.reshape(PROMPT, KVH * HD), grad_v.reshape(PROMPT, KVH * HD))
```

```python
import functools
import math

import jax
import jax.numpy as jnp
from jax import lax
from jax.experimental import pallas as pl
from jax.experimental.pallas import tpu as pltpu
from jax.sharding import PartitionSpec as P

HD = 128
KVH = 2
CORES = 2
NY = 4
MESH = pl.DeviceIdType.MESH
BF16 = jnp.bfloat16
F32 = jnp.float32


def kernel(
    geo,
    len_ref,
    q_hbm,
    g_hbm,
    k_ref,
    v_ref,
    gq_hbm,
    gk_ref,
    gv_ref,
    q_v,
    g_v,
    swap_tx,
    swap_rx,
    pack_f,
    pack,
    near,
    kv,
    p_t,
    ds_t,
    acc,
    acc_rx,
    pl_tx,
    pl_rx,
    z_tx,
    z_rx,
    x_tx,
    x_rx,
    gq_v,
    in_sem,
    out_sem,
    swap_ss,
    swap_rs,
    near_ss,
    near_rs,
    gat_ss,
    gat_rs,
    sib_ss,
    sib_rs,
    acc_ss,
    acc_rs,
    pl_ss,
    pl_rs,
    z_ss,
    z_rs,
    x_ss,
    x_rs,
):
    nx, ny, zl, zh = geo
    nz = zl * zh
    half = nz // KVH
    nt = half // nx
    plane = nx * ny
    rows = q_v.shape[0]
    width = q_v.shape[1]
    heads = width // HD
    blk = kv.shape[3]
    span = CORES * plane * blk
    scale = 1.0 / math.sqrt(HD)

    x = lax.axis_index("resp")
    ep = lax.axis_index("ep")
    kvi = lax.axis_index("kv")
    y, z_lo = lax.div(ep, zl), lax.rem(ep, zl)
    z_hi, c = lax.div(kvi, CORES), lax.rem(kvi, CORES)
    z = z_hi * zl + z_lo
    me = x * ny + y
    sib = 1 - c
    zhalf = lax.div(z, half)

    def dev(xx, yy, zz, cc):
        return (xx, yy * zl + lax.rem(zz, zl), lax.div(zz, zl) * CORES + cc)

    def rcopy(src, dst, ss, rs, device):
        return pltpu.make_async_remote_copy(
            src_ref=src, dst_ref=dst, send_sem=ss, recv_sem=rs, device_id=device, device_id_type=MESH
        )

    def to_z(i):
        return half * c + nx * i + lax.rem(z + x, nx)

    def from_z(i):
        return half * c + nx * i + lax.rem(z - x + nx, nx)

    def plane_dev(slot):
        return dev(lax.div(slot, ny), lax.rem(slot, ny), z, c)

    my_t = lax.div(lax.rem(z, half), nx)
    sib_dev = dev(x, y, z, sib)

    q_in = pltpu.make_async_copy(
        q_hbm.at[0, :, pl.ds(pl.multiple_of(kvi * width, width), width)], q_v, in_sem.at[0]
    )
    g_in = pltpu.make_async_copy(
        g_hbm.at[0, :, pl.ds(pl.multiple_of(kvi * width, width), width)], g_v, in_sem.at[1]
    )
    q_in.start()
    g_in.start()

    barrier = pltpu.get_barrier_semaphore()

    def signal(device):
        pl.semaphore_signal(barrier, inc=1, device_id=device, device_id_type=MESH)

    signal(sib_dev)

    def signal_plane(o, carry):
        signal(plane_dev(lax.rem(me + o, plane)))
        return carry

    lax.fori_loop(1, plane, signal_plane, 0)

    def signal_x(o, carry):
        signal(dev(lax.rem(x + o, nx), y, z, sib))
        return carry

    lax.fori_loop(1, nx, signal_x, 0)

    def is_self(zz):
        return jnp.logical_and(zz == z, zhalf == c)

    def signal_z(i, carry):
        @pl.when(jnp.logical_not(is_self(to_z(i))))
        def _():
            signal(dev(x, y, to_z(i), zhalf))

        @pl.when(jnp.logical_not(is_self(from_z(i))))
        def _():
            signal(dev(x, y, from_z(i), zhalf))

        return carry

    lax.fori_loop(0, nt, signal_z, 0)
    has_self = jnp.logical_and(x == 0, zhalf == c)
    total = 1 + (plane - 1) + (nx - 1) + 2 * nt
    pl.semaphore_wait(barrier, total - jnp.where(has_self, 2, 0))

    def head_of(ref, h):
        value = ref[...].astype(F32)
        return jnp.where(h == 0, value[:, :HD], value[:, HD:])

    lanes = k_ref.shape[0]
    swap_tx[0:lanes] = head_of(k_ref, sib)
    swap_tx[lanes:] = head_of(v_ref, sib)
    swap = rcopy(swap_tx, swap_rx, swap_ss, swap_rs, sib_dev)
    swap.start()
    pack_f[pl.ds(lanes * c, lanes)] = head_of(k_ref, c)
    pack_f[pl.ds(lanes * (2 + c), lanes)] = head_of(v_ref, c)
    swap.wait()
    pack_f[pl.ds(lanes * sib, lanes)] = swap_rx[0:lanes]
    pack_f[pl.ds(lanes * (2 + sib), lanes)] = swap_rx[lanes:]
    pack[...] = pack_f[...].astype(BF16)

    def near_copy(i):
        return rcopy(pack, near.at[my_t], near_ss.at[i], near_rs.at[my_t], dev(x, y, to_z(i), zhalf))

    def near_send(i, carry):
        own = is_self(to_z(i))

        @pl.when(own)
        def _():
            near[my_t] = pack[...]

        @pl.when(jnp.logical_not(own))
        def _():
            near_copy(i).start()

        return carry

    lax.fori_loop(0, nt, near_send, 0)

    def near_recv(i, carry):
        @pl.when(jnp.logical_not(is_self(from_z(i))))
        def _():
            rcopy(pack, near.at[i], near_ss.at[0], near_rs.at[i], sib_dev).wait_recv()

        return carry

    lax.fori_loop(0, nt, near_recv, 0)

    got = near[...].astype(F32).reshape(nt, 2, 2 * lanes, HD)
    kv[c, me, 0] = got[:, 0].reshape(blk, HD).astype(BF16)
    kv[c, me, 1] = got[:, 1].reshape(blk, HD).astype(BF16)

    def gather_send(o, carry):
        rcopy(
            kv.at[c, me],
            kv.at[c, me],
            gat_ss.at[o],
            gat_rs.at[me],
            plane_dev(lax.rem(me + o, plane)),
        ).start()
        return carry

    lax.fori_loop(1, plane, gather_send, 0)

    def gather_recv(o, carry):
        slot = lax.rem(me - o + plane, plane)
        rcopy(kv.at[c, me], kv.at[c, slot], gat_ss.at[0], gat_rs.at[slot], sib_dev).wait_recv()
        return carry

    lax.fori_loop(1, plane, gather_recv, 0)
    share = rcopy(kv.at[c], kv.at[c], sib_ss, sib_rs, sib_dev)
    share.start()
    share.wait_send()
    rcopy(kv.at[sib], kv.at[sib], sib_ss, sib_rs, sib_dev).wait_recv()

    q_in.wait()
    g_in.wait()

    keys = kv[:, :, 0].reshape(span, HD)
    values = kv[:, :, 1].reshape(span, HD)
    own_length = len_ref[x]
    valid = ep * rows + lax.broadcasted_iota(jnp.int32, (rows, HD), 0) < own_length
    factor = scale * math.log2(math.e)
    for h in range(heads):
        cols = slice(h * HD, (h + 1) * HD)
        g_v[:, cols] = jnp.where(valid, g_v[:, cols], jnp.zeros((), BF16))
        q_h = q_v[:, cols]
        g_h = g_v[:, cols]
        s = lax.dot_general(keys, q_h, (((1,), (1,)), ((), ())), preferred_element_type=F32)
        top = jnp.max(s, axis=0, keepdims=True)
        e = jnp.exp2((s - top) * factor)
        prob = e * (1.0 / jnp.sum(e, axis=0, keepdims=True))
        p_t[:, h * rows : (h + 1) * rows] = prob.astype(BF16)
        dp = lax.dot_general(values, g_h, (((1,), (1,)), ((), ())), preferred_element_type=F32)
        delta = jnp.sum(prob * dp, axis=0, keepdims=True)
        ds_t[:, h * rows : (h + 1) * rows] = (prob * (dp - delta)).astype(BF16)

    def stacked(ref):
        return jnp.concatenate([ref[:, h * HD : (h + 1) * HD] for h in range(heads)], axis=0)

    acc[1] = jnp.dot(p_t[...], stacked(g_v), preferred_element_type=F32).reshape(CORES, span // 2, HD)
    acc_v = rcopy(acc.at[1, sib], acc_rx.at[1], acc_ss.at[1], acc_rs.at[1], sib_dev)
    acc_v.start()
    acc[0] = jnp.dot(ds_t[...], stacked(q_v), preferred_element_type=F32).reshape(CORES, span // 2, HD)
    acc_k = rcopy(acc.at[0, sib], acc_rx.at[0], acc_ss.at[0], acc_rs.at[0], sib_dev)
    acc_k.start()

    def plane_send(part):
        both = (acc[part, c] + acc_rx[part]).astype(BF16)
        pl_tx[part] = both.reshape(plane, blk, HD)
        pl_rx[part, me] = pl_tx[part, me]

        def send(o, carry):
            to = lax.rem(me + o, plane)
            rcopy(
                pl_tx.at[part, to], pl_rx.at[part, me], pl_ss.at[part, o], pl_rs.at[part, me], plane_dev(to)
            ).start()
            return carry

        lax.fori_loop(1, plane, send, 0)

    acc_v.wait()
    plane_send(1)
    acc_k.wait()
    plane_send(0)

    keys_t = keys.T
    gq_t = jnp.dot(keys_t, ds_t[...], preferred_element_type=F32) * scale
    for h in range(heads):
        gq_v[:, h * HD : (h + 1) * HD] = gq_t[:, h * rows : (h + 1) * rows].T
    gq_out = pltpu.make_async_copy(gq_v, gq_hbm.at[0], out_sem)
    gq_out.start()

    def plane_recv(part):
        def recv(o, carry):
            slot = lax.rem(me - o + plane, plane)
            rcopy(
                pl_tx.at[part, slot], pl_rx.at[part, slot], pl_ss.at[part, 0], pl_rs.at[part, slot], sib_dev
            ).wait_recv()
            return carry

        lax.fori_loop(1, plane, recv, 0)
        return jnp.sum(pl_rx[part].astype(F32), axis=0).reshape(nt, 1, 2 * lanes, HD)

    v_sum = plane_recv(1)
    k_sum = plane_recv(0)
    z_tx[...] = jnp.concatenate([k_sum, v_sum], axis=1).reshape(nt, 4 * lanes, HD).astype(BF16)

    def z_send(i, carry):
        own = is_self(from_z(i))

        @pl.when(own)
        def _():
            z_rx[my_t] = z_tx[i]

        @pl.when(jnp.logical_not(own))
        def _():
            rcopy(
                z_tx.at[i], z_rx.at[my_t], z_ss.at[i], z_rs.at[my_t], dev(x, y, from_z(i), zhalf)
            ).start()

        return carry

    lax.fori_loop(0, nt, z_send, 0)

    def z_recv(i, carry):
        @pl.when(jnp.logical_not(is_self(to_z(i))))
        def _():
            rcopy(z_tx.at[i], z_rx.at[i], z_ss.at[0], z_rs.at[i], sib_dev).wait_recv()

        return carry

    lax.fori_loop(0, nt, z_recv, 0)

    z_sum = jnp.sum(z_rx[...].astype(F32), axis=0)
    for core in range(CORES):
        x_tx[core, 0:lanes] = z_sum[core * lanes : (core + 1) * lanes]
        x_tx[core, lanes:] = z_sum[(2 + core) * lanes : (3 + core) * lanes]
    x_rx[x, c] = x_tx[c]

    def x_send(o, carry):
        dx, core = lax.div(o, CORES), lax.rem(c + lax.rem(o, CORES), CORES)
        rcopy(
            x_tx.at[core], x_rx.at[x, c], x_ss.at[o], x_rs.at[x, c], dev(lax.rem(x + dx, nx), y, z, core)
        ).start()
        return carry

    lax.fori_loop(1, CORES * nx, x_send, 0)

    def x_recv(o, carry):
        dx, core = lax.div(o, CORES), lax.rem(c + lax.rem(o, CORES), CORES)
        slot = lax.rem(x - dx + nx, nx)
        rcopy(x_tx.at[0], x_rx.at[slot, core], x_ss.at[0], x_rs.at[slot, core], sib_dev).wait_recv()
        return carry

    lax.fori_loop(1, CORES * nx, x_recv, 0)
    for core in range(CORES):
        done = jnp.sum(x_rx[:, core], axis=0)
        gk_ref[:, core * HD : (core + 1) * HD] = done[:lanes] * scale
        gv_ref[:, core * HD : (core + 1) * HD] = done[lanes:]

    def near_done(i, carry):
        @pl.when(jnp.logical_not(is_self(to_z(i))))
        def _():
            near_copy(i).wait_send()

        @pl.when(jnp.logical_not(is_self(from_z(i))))
        def _():
            rcopy(z_tx.at[i], z_rx.at[0], z_ss.at[i], z_rs.at[0], sib_dev).wait_send()

        return carry

    lax.fori_loop(0, nt, near_done, 0)

    def plane_done(o, carry):
        rcopy(kv.at[c, me], kv.at[c, me], gat_ss.at[o], gat_rs.at[0], sib_dev).wait_send()
        for part in range(2):
            rcopy(
                pl_tx.at[part, 0], pl_rx.at[part, 0], pl_ss.at[part, o], pl_rs.at[part, 0], sib_dev
            ).wait_send()
        return carry

    lax.fori_loop(1, plane, plane_done, 0)

    def x_done(o, carry):
        rcopy(x_tx.at[0], x_rx.at[0, 0], x_ss.at[o], x_rs.at[0, 0], sib_dev).wait_send()
        return carry

    lax.fori_loop(1, CORES * nx, x_done, 0)
    gq_out.wait()


def make(mesh, ny):
    nx = mesh.shape["resp"]
    zl = mesh.shape["ep"] // ny
    zh = mesh.shape["kv"] // CORES
    geo = (nx, ny, zl, zh)
    plane = nx * ny
    nt = zl * zh // KVH // nx

    def body(lengths, queries, grad_out, prompt_keys, prompt_values):
        rows = queries.shape[1]
        width = queries.shape[2] // mesh.shape["kv"]
        lanes = prompt_keys.shape[0]
        blk = nt * CORES * lanes
        span = CORES * plane * blk
        dma = pltpu.SemaphoreType.DMA
        vmem = pl.BlockSpec(memory_space=pltpu.VMEM)
        hbm = pl.BlockSpec(memory_space=pltpu.HBM)
        return pl.pallas_call(
            functools.partial(kernel, geo),
            out_shape=(
                jax.ShapeDtypeStruct((1, rows, width), F32),
                jax.ShapeDtypeStruct(prompt_keys.shape, F32),
                jax.ShapeDtypeStruct(prompt_values.shape, F32),
            ),
            in_specs=[pl.BlockSpec(memory_space=pltpu.SMEM), hbm, hbm, vmem, vmem],
            out_specs=(hbm, vmem, vmem),
            scratch_shapes=[
                pltpu.VMEM((rows, width), BF16),
                pltpu.VMEM((rows, width), BF16),
                pltpu.VMEM((2 * lanes, HD), F32),
                pltpu.VMEM((2 * lanes, HD), F32),
                pltpu.VMEM((4 * lanes, HD), F32),
                pltpu.VMEM((4 * lanes, HD), BF16),
                pltpu.VMEM((nt, 4 * lanes, HD), BF16),
                pltpu.VMEM((CORES, plane, 2, blk, HD), BF16),
                pltpu.VMEM((span, rows * width // HD), BF16),
                pltpu.VMEM((span, rows * width // HD), BF16),
                pltpu.VMEM((2, CORES, span // 2, HD), F32),
                pltpu.VMEM((2, span // 2, HD), F32),
                pltpu.VMEM((2, plane, blk, HD), BF16),
                pltpu.VMEM((2, plane, blk, HD), BF16),
                pltpu.VMEM((nt, 4 * lanes, HD), BF16),
                pltpu.VMEM((nt, 4 * lanes, HD), BF16),
                pltpu.VMEM((CORES, 2 * lanes, HD), F32),
                pltpu.VMEM((nx, CORES, 2 * lanes, HD), F32),
                pltpu.VMEM((rows, width), F32),
                dma((2,)),
                dma,
                dma,
                dma,
                dma((nt,)),
                dma((nt,)),
                dma((plane,)),
                dma((plane,)),
                dma,
                dma,
                dma((2,)),
                dma((2,)),
                dma((2, plane)),
                dma((2, plane)),
                dma((nt,)),
                dma((nt,)),
                dma((CORES * nx,)),
                dma((nx, CORES)),
            ],
            compiler_params=pltpu.CompilerParams(
                collective_id=0, has_side_effects=True, vmem_limit_bytes=40 * 1024 * 1024
            ),
        )(lengths, queries, grad_out, prompt_keys, prompt_values)

    return jax.shard_map(
        body,
        mesh=mesh,
        in_specs=(
            P(),
            P("resp", "ep", None),
            P("resp", "ep", None),
            P(("ep", "kv"), None),
            P(("ep", "kv"), None),
        ),
        out_specs=(P("resp", "ep", "kv"), P(("ep", "kv"), None), P(("ep", "kv"), None)),
        check_vma=False,
    )


def solution(mesh):
    return make(mesh, NY)
```

```python
import functools
import math

import jax
import jax.numpy as jnp
from jax import lax
from jax.experimental import pallas as pl
from jax.experimental.pallas import tpu as pltpu
from jax.sharding import PartitionSpec as P

HD = 128
KVH = 2
CORES = 2
NY = 4
MESH = pl.DeviceIdType.MESH
BF16 = jnp.bfloat16
F32 = jnp.float32


def kernel(
    geo,
    len_hbm,
    q_hbm,
    g_hbm,
    k_hbm,
    v_hbm,
    gq_hbm,
    gk_hbm,
    gv_hbm,
    len_s,
    k_v,
    v_v,
    q_v,
    g_v,
    q_s,
    g_s,
    pack_f,
    pack,
    near,
    rows_f,
    kb,
    vb,
    p_t,
    ds_t,
    acc,
    acc_rx,
    one_tx,
    one_rx,
    two_tx,
    two_rx,
    z_tx,
    z_rx,
    x_tx,
    x_rx,
    gq_v,
    gk_v,
    gv_v,
    in_sem,
    out_sem,
    near_ss,
    near_rs,
    kb_ss,
    kb_rs,
    vb_ss,
    vb_rs,
    sib_ss,
    sib_rs,
    acc_ss,
    acc_rs,
    one_ss,
    one_rs,
    two_ss,
    two_rs,
    z_ss,
    z_rs,
    x_ss,
    x_rs,
):
    nx, ny, zl, zh = geo
    nz = zl * zh
    half = nz // KVH
    far = nz // 4
    rows = q_v.shape[0]
    width = q_v.shape[1]
    heads = width // HD
    lanes = k_v.shape[0]
    blk = kb.shape[3]
    span = CORES * nx * ny * blk
    scale = 1.0 / math.sqrt(HD)

    x = lax.axis_index("resp")
    ep = lax.axis_index("ep")
    kvi = lax.axis_index("kv")
    y, z_lo = lax.div(ep, zl), lax.rem(ep, zl)
    z_hi, c = lax.div(kvi, CORES), lax.rem(kvi, CORES)
    z = z_hi * zl + z_lo

    def at_z(offset):
        zz = lax.rem(z + offset + nz, nz)
        return (x, y * zl + lax.rem(zz, zl), lax.div(zz, zl) * CORES + c)

    def at_x(offset):
        return (lax.rem(x + offset + nx, nx), ep, kvi)

    def at_y(offset):
        return (x, lax.rem(y + offset + ny, ny) * zl + z_lo, kvi)

    sib = (x, ep, z_hi * CORES + 1 - c)

    first = jnp.where(x == 0, nx, x)
    second = first + nx
    direct = [first, second, -first, -second]
    relayed = [first + far, second + far, -first - far, jnp.where(x == 0, 0, -second - far)]
    offsets = direct + relayed
    count = len(offsets)

    barrier = pltpu.get_barrier_semaphore()
    peers = [at_z(o) for o in (-far, far, -second, second, -first, first)]
    peers += [at_y(o) for o in range(1, ny)] + [at_x(o) for o in range(1, nx)] + [sib]
    for peer in peers:
        pl.semaphore_signal(barrier, inc=1, device_id=peer, device_id_type=MESH)

    copies = [
        pltpu.make_async_copy(k_hbm, k_v, in_sem.at[0]),
        pltpu.make_async_copy(v_hbm, v_v, in_sem.at[1]),
        pltpu.make_async_copy(len_hbm, len_s, in_sem.at[2]),
    ]
    own = pl.ds(pl.multiple_of(kvi * width, width), width)
    copies.append(pltpu.make_async_copy(q_hbm.at[0, :, own], q_v, in_sem.at[3]))
    copies.append(pltpu.make_async_copy(g_hbm.at[0, :, own], g_v, in_sem.at[4]))
    for copy in copies:
        copy.start()

    sent = []

    def send(src, dst, ss, rs, device):
        copy = pltpu.make_async_remote_copy(
            src_ref=src, dst_ref=dst, send_sem=ss, recv_sem=rs, device_id=device, device_id_type=MESH
        )
        copy.start()
        sent.append(copy)
        return copy

    copies[0].wait()
    copies[1].wait()
    for h in range(KVH):
        for part, ref in enumerate((k_v, v_v)):
            at = (2 * h + part) * lanes
            pack_f[at : at + lanes] = ref[:, h * HD : (h + 1) * HD].astype(F32)
    pack[...] = pack_f[...].astype(BF16)
    pl.semaphore_wait(barrier, len(peers))

    z_in = [send(pack, near.at[i], near_ss.at[i], near_rs.at[i], at_z(-direct[i])) for i in (1, 3, 0, 2)]
    z_in[0].wait_recv()
    z_in[2].wait_recv()
    fwd_up = send(near.at[0:2], near.at[4:6], near_ss.at[4], near_rs.at[4], at_z(-far))
    z_in[1].wait_recv()
    z_in[3].wait_recv()
    fwd_down = send(near.at[2:4], near.at[6:8], near_ss.at[5], near_rs.at[5], at_z(far))

    for copy in copies[2:]:
        copy.wait()
    valid = ep * rows + lax.broadcasted_iota(jnp.int32, (rows, HD), 0) < len_s[x]
    for h in range(heads):
        cols = slice(h * HD, (h + 1) * HD)
        at = slice(h * rows, (h + 1) * rows)
        q_s[at] = q_v[:, cols]
        g_s[at] = jnp.where(valid, g_v[:, cols], jnp.zeros((), BF16))

    fwd_up.wait_recv()
    fwd_down.wait_recv()

    mine = lax.div(z, half)
    for i in range(count):
        packet = near[i].astype(F32)
        if i == count - 1:
            packet = jnp.where(x == 0, pack_f[...], packet)
        packet = jnp.where(mine == 0, packet[: 2 * lanes], packet[2 * lanes :])
        rows_f[0, i * lanes : (i + 1) * lanes] = packet[:lanes]
        rows_f[1, i * lanes : (i + 1) * lanes] = packet[lanes:]
    kb[0, 0, 0] = rows_f[0].astype(BF16)
    vb[0, 0, 0] = rows_f[1].astype(BF16)

    k_one = [send(kb.at[0, 0, 0], kb.at[0, 0, o], kb_ss.at[0, o], kb_rs.at[0, o], at_x(o)) for o in range(1, nx)]
    v_one = [send(vb.at[0, 0, 0], vb.at[0, o, 0], vb_ss.at[0, o], vb_rs.at[0, o], at_y(o)) for o in range(1, ny)]
    for copy in k_one:
        copy.wait_recv()
    k_two = [send(kb.at[0, 0], kb.at[0, o], kb_ss.at[1, o], kb_rs.at[1, o], at_y(o)) for o in range(1, ny)]
    for copy in v_one:
        copy.wait_recv()
    v_two = [
        send(vb.at[0, :, 0], vb.at[0, :, o], vb_ss.at[1, o], vb_rs.at[1, o], at_x(o)) for o in range(1, nx)
    ]
    shared = [
        send(kb.at[0, 0], kb.at[1, 0], sib_ss.at[0], sib_rs.at[0], sib),
        send(vb.at[0, :, 0], vb.at[1, :, 0], sib_ss.at[1], sib_rs.at[1], sib),
    ]
    for copy in k_two:
        copy.wait_recv()
    shared.append(send(kb.at[0, 1:ny], kb.at[1, 1:ny], sib_ss.at[2], sib_rs.at[2], sib))
    for copy in v_two:
        copy.wait_recv()
    shared.append(send(vb.at[0, :, 1:nx], vb.at[1, :, 1:nx], sib_ss.at[3], sib_rs.at[3], sib))
    for copy in shared:
        copy.wait_recv()

    keys = kb[...].reshape(span, HD)
    values = vb[...].reshape(span, HD)
    factor = scale * math.log2(math.e)
    for h in range(heads):
        at = slice(h * rows, (h + 1) * rows)
        s = lax.dot_general(keys, q_s[at], (((1,), (1,)), ((), ())), preferred_element_type=F32)
        top = jnp.max(s, axis=0, keepdims=True)
        e = jnp.exp2((s - top) * factor)
        prob = e * (1.0 / jnp.sum(e, axis=0, keepdims=True))
        p_t[:, at] = prob.astype(BF16)
        dp = lax.dot_general(values, g_s[at], (((1,), (1,)), ((), ())), preferred_element_type=F32)
        delta = jnp.sum(prob * dp, axis=0, keepdims=True)
        ds_t[:, at] = (prob * (dp - delta)).astype(BF16)

    def partial(part, weights, operand):
        total = jnp.dot(weights[...], operand[...], preferred_element_type=F32)
        acc[part] = total.reshape(CORES, ny, nx, blk, HD)
        return send(acc.at[part, 1], acc_rx.at[part], acc_ss.at[part], acc_rs.at[part], sib)

    v_acc = partial(1, p_t, g_s)
    k_acc = partial(0, ds_t, q_s)

    v_acc.wait_recv()
    v_all = acc[1, 0] + acc_rx[1]
    for o in range(1, nx):
        one_tx[1, o] = v_all[:, o].astype(BF16)
    v_one = [
        send(one_tx.at[1, o], one_rx.at[1, o], one_ss.at[1, o], one_rs.at[1, o], at_x(-o)) for o in range(1, nx)
    ]
    acc[1, 0, :, 0] = v_all[:, 0]
    k_acc.wait_recv()
    k_all = acc[0, 0] + acc_rx[0]
    for o in range(1, ny):
        one_tx[0, o] = k_all[o].astype(BF16)
    k_one = [
        send(one_tx.at[0, o], one_rx.at[0, o], one_ss.at[0, o], one_rs.at[0, o], at_y(-o)) for o in range(1, ny)
    ]
    acc[0, 0, 0] = k_all[0]

    for copy in v_one:
        copy.wait_recv()
    v_half = acc[1, 0, :, 0]
    for o in range(1, nx):
        v_half += one_rx[1, o].astype(F32)
    two_tx[1] = v_half
    v_two = [
        send(two_tx.at[1, o], two_rx.at[1, o], two_ss.at[1, o], two_rs.at[1, o], at_y(-o)) for o in range(1, ny)
    ]
    for copy in k_one:
        copy.wait_recv()
    k_half = acc[0, 0, 0]
    for o in range(1, ny):
        k_half += one_rx[0, o].astype(F32)
    two_tx[0] = k_half
    k_two = [
        send(two_tx.at[0, o], two_rx.at[0, o], two_ss.at[0, o], two_rs.at[0, o], at_x(-o)) for o in range(1, nx)
    ]
    for copy in v_two:
        copy.wait_recv()
    for copy in k_two:
        copy.wait_recv()
    for part, size in ((0, nx), (1, ny)):
        total = two_tx[part, 0]
        for o in range(1, size):
            total += two_rx[part, o]
        rows_f[part] = total
    for i in range(count):
        for part in range(2):
            z_tx[i, part * lanes : (part + 1) * lanes] = rows_f[part, i * lanes : (i + 1) * lanes]

    def z_copy(i):
        return pltpu.make_async_remote_copy(
            src_ref=z_tx.at[i],
            dst_ref=z_rx.at[i],
            send_sem=z_ss.at[i],
            recv_sem=z_rs.at[i],
            device_id=at_z(offsets[i]),
            device_id_type=MESH,
        )

    for i in (5, 4, 6, 1, 3, 0, 2):
        z_copy(i).start()

    @pl.when(x != 0)
    def _():
        z_copy(count - 1).start()

    @pl.when(x == 0)
    def _():
        z_rx[count - 1] = z_tx[count - 1]

    gq_t = jnp.dot(keys.T, ds_t[...], preferred_element_type=F32) * scale
    for h in range(heads):
        gq_v[:, h * HD : (h + 1) * HD] = gq_t[:, h * rows : (h + 1) * rows].T
    gq_out = pltpu.make_async_copy(gq_v, gq_hbm.at[0], out_sem.at[0])
    gq_out.start()

    for i in range(count - 1):
        z_copy(i).wait_recv()

    @pl.when(x != 0)
    def _():
        z_copy(count - 1).wait_recv()

    for h in range(KVH):
        total = jnp.zeros((2 * lanes, HD), F32)
        for i in range(count):
            source = lax.rem(z - offsets[i] + nz, nz)
            total += jnp.where(lax.div(source, half) == h, z_rx[i], 0.0)
        x_tx[h] = total
    last = [send(x_tx, x_rx.at[o], x_ss.at[o], x_rs.at[o], at_x(o)) for o in range(1, nx)]
    for copy in last:
        copy.wait_recv()
    for h in range(KVH):
        total = x_tx[h]
        for o in range(1, nx):
            total += x_rx[o, h]
        gk_v[:, h * HD : (h + 1) * HD] = total[:lanes] * scale
        gv_v[:, h * HD : (h + 1) * HD] = total[lanes:]
    gk_out = pltpu.make_async_copy(gk_v, gk_hbm, out_sem.at[1])
    gv_out = pltpu.make_async_copy(gv_v, gv_hbm, out_sem.at[2])
    gk_out.start()
    gv_out.start()

    for copy in sent:
        copy.wait_send()
    for i in range(count - 1):
        z_copy(i).wait_send()

    @pl.when(x != 0)
    def _():
        z_copy(count - 1).wait_send()

    gq_out.wait()
    gk_out.wait()
    gv_out.wait()


def hand_over(gq, gk, gv, gq_out, gk_out, gv_out):
    gq_out[...] = gq[...]
    gk_out[...] = gk[...]
    gv_out[...] = gv[...]


def make(mesh, ny):
    nx = mesh.shape["resp"]
    zl = mesh.shape["ep"] // ny
    zh = mesh.shape["kv"] // CORES
    geo = (nx, ny, zl, zh)
    count = zl * zh // nx

    def body(lengths, queries, grad_out, prompt_keys, prompt_values):
        rows = queries.shape[1]
        width = queries.shape[2] // mesh.shape["kv"]
        lanes = prompt_keys.shape[0]
        blk = count * lanes
        span = CORES * nx * ny * blk
        stacked = rows * width // HD
        side = max(nx, ny)
        dma = pltpu.SemaphoreType.DMA
        hbm = pl.BlockSpec(memory_space=pltpu.HBM)
        out_shape = (
            jax.ShapeDtypeStruct((1, rows, width), F32),
            jax.ShapeDtypeStruct(prompt_keys.shape, F32),
            jax.ShapeDtypeStruct(prompt_values.shape, F32),
        )
        grads = pl.pallas_call(
            functools.partial(kernel, geo),
            out_shape=out_shape,
            in_specs=[hbm] * 5,
            out_specs=(hbm, hbm, hbm),
            scratch_shapes=[
                pltpu.SMEM(lengths.shape, jnp.int32),
                pltpu.VMEM(prompt_keys.shape, BF16),
                pltpu.VMEM(prompt_values.shape, BF16),
                pltpu.VMEM((rows, width), BF16),
                pltpu.VMEM((rows, width), BF16),
                pltpu.VMEM((stacked, HD), BF16),
                pltpu.VMEM((stacked, HD), BF16),
                pltpu.VMEM((4 * lanes, HD), F32),
                pltpu.VMEM((4 * lanes, HD), BF16),
                pltpu.VMEM((count, 4 * lanes, HD), BF16),
                pltpu.VMEM((2, blk, HD), F32),
                pltpu.VMEM((CORES, ny, nx, blk, HD), BF16),
                pltpu.VMEM((CORES, ny, nx, blk, HD), BF16),
                pltpu.VMEM((span, stacked), BF16),
                pltpu.VMEM((span, stacked), BF16),
                pltpu.VMEM((2, CORES, ny, nx, blk, HD), F32),
                pltpu.VMEM((2, ny, nx, blk, HD), F32),
                pltpu.VMEM((2, side, side, blk, HD), BF16),
                pltpu.VMEM((2, side, side, blk, HD), BF16),
                pltpu.VMEM((2, side, blk, HD), F32),
                pltpu.VMEM((2, side, blk, HD), F32),
                pltpu.VMEM((count, 2 * lanes, HD), F32),
                pltpu.VMEM((count, 2 * lanes, HD), F32),
                pltpu.VMEM((KVH, 2 * lanes, HD), F32),
                pltpu.VMEM((nx, KVH, 2 * lanes, HD), F32),
                pltpu.VMEM((rows, width), F32),
                pltpu.VMEM(prompt_keys.shape, F32),
                pltpu.VMEM(prompt_values.shape, F32),
                dma((5,)),
                dma((3,)),
                dma((6,)),
                dma((6,)),
                dma((2, side)),
                dma((2, side)),
                dma((2, side)),
                dma((2, side)),
                dma((4,)),
                dma((4,)),
                dma((2,)),
                dma((2,)),
                dma((2, side)),
                dma((2, side)),
                dma((2, side)),
                dma((2, side)),
                dma((count,)),
                dma((count,)),
                dma((nx,)),
                dma((nx,)),
            ],
            compiler_params=pltpu.CompilerParams(
                collective_id=0, has_side_effects=True, vmem_limit_bytes=60 * 1024 * 1024
            ),
        )(lengths, queries, grad_out, prompt_keys, prompt_values)
        return pl.pallas_call(hand_over, out_shape=out_shape)(*grads)

    return jax.shard_map(
        body,
        mesh=mesh,
        in_specs=(
            P(),
            P("resp", "ep", None),
            P("resp", "ep", None),
            P(("ep", "kv"), None),
            P(("ep", "kv"), None),
        ),
        out_specs=(P("resp", "ep", "kv"), P(("ep", "kv"), None), P(("ep", "kv"), None)),
        check_vma=False,
    )


def solution(mesh):
    return make(mesh, NY)
```

```python
import functools
import math

import jax
import jax.numpy as jnp
from jax import lax
from jax.experimental import pallas as pl
from jax.experimental.pallas import tpu as pltpu
from jax.sharding import PartitionSpec as P

HD = 128
KVH = 2
CORES = 2
NY = 4
MESH = pl.DeviceIdType.MESH
BF16 = jnp.bfloat16
F32 = jnp.float32


def kernel(
    geo,
    len_hbm,
    q_hbm,
    g_hbm,
    k_hbm,
    v_hbm,
    gq_hbm,
    gk_hbm,
    gv_hbm,
    len_s,
    k_v,
    v_v,
    q_v,
    g_v,
    q_s,
    g_s,
    pack_f,
    pack,
    near,
    rows_f,
    kv,
    s_f,
    dp_f,
    p_t,
    ds_t,
    acc,
    acc_rx,
    kept,
    one_tx,
    one_rx,
    two_tx,
    two_rx,
    z_tx,
    z_rx,
    x_tx,
    x_rx,
    gq_v,
    gk_v,
    gv_v,
    in_sem,
    out_sem,
    near_ss,
    near_rs,
    kv_ss,
    kv_rs,
    sib_ss,
    sib_rs,
    acc_ss,
    acc_rs,
    one_ss,
    one_rs,
    two_ss,
    two_rs,
    z_ss,
    z_rs,
    x_ss,
    x_rs,
):
    nx, ny, zl, zh = geo
    nz = zl * zh
    half = nz // KVH
    far = nz // 4
    rows = q_v.shape[0]
    width = q_v.shape[1]
    heads = width // HD
    lanes = k_v.shape[0]
    part_rows = kv.shape[5]
    span = CORES * 2 * nx * ny * part_rows
    mid = span // 2
    scale = 1.0 / math.sqrt(HD)

    x = lax.axis_index("resp")
    ep = lax.axis_index("ep")
    kvi = lax.axis_index("kv")
    y, z_lo = lax.div(ep, zl), lax.rem(ep, zl)
    z_hi, c = lax.div(kvi, CORES), lax.rem(kvi, CORES)
    z = z_hi * zl + z_lo

    def at_z(offset):
        zz = lax.rem(z + offset + nz, nz)
        return (x, y * zl + lax.rem(zz, zl), lax.div(zz, zl) * CORES + c)

    def at_x(offset):
        return (lax.rem(x + offset + nx, nx), ep, kvi)

    def at_y(offset):
        return (x, lax.rem(y + offset + ny, ny) * zl + z_lo, kvi)

    def in_plane(ox, oy):
        return (lax.rem(x + ox, nx), lax.rem(y + oy, ny) * zl + z_lo, kvi)

    sib = (x, ep, z_hi * CORES + 1 - c)

    plane = [(ox, oy) for ox in range(nx) for oy in range(ny) if ox or oy]
    plane.sort(key=lambda o: -min(o[0], nx - o[0]) - min(o[1], ny - o[1]))

    first = jnp.where(x == 0, nx, x)
    second = first + nx
    direct = [first, second, -first, -second]
    relayed = [first + far, second + far, -first - far, jnp.where(x == 0, 0, -second - far)]
    offsets = direct + relayed
    count = len(offsets)

    barrier = pltpu.get_barrier_semaphore()
    peers = [at_z(o) for o in (-far, far, -second, second, -first, first)]
    peers += [in_plane(*o) for o in plane] + [sib]
    for peer in peers:
        pl.semaphore_signal(barrier, inc=1, device_id=peer, device_id_type=MESH)

    copies = [
        pltpu.make_async_copy(k_hbm, k_v, in_sem.at[0]),
        pltpu.make_async_copy(v_hbm, v_v, in_sem.at[1]),
        pltpu.make_async_copy(len_hbm, len_s, in_sem.at[2]),
    ]
    own = pl.ds(pl.multiple_of(kvi * width, width), width)
    copies.append(pltpu.make_async_copy(q_hbm.at[0, :, own], q_v, in_sem.at[3]))
    copies.append(pltpu.make_async_copy(g_hbm.at[0, :, own], g_v, in_sem.at[4]))
    for copy in copies:
        copy.start()

    sent = []

    def send(src, dst, ss, rs, device):
        copy = pltpu.make_async_remote_copy(
            src_ref=src, dst_ref=dst, send_sem=ss, recv_sem=rs, device_id=device, device_id_type=MESH
        )
        copy.start()
        sent.append(copy)
        return copy

    copies[0].wait()
    copies[1].wait()
    for h in range(KVH):
        for part, ref in enumerate((k_v, v_v)):
            at = (2 * h + part) * lanes
            pack_f[at : at + lanes] = ref[:, h * HD : (h + 1) * HD].astype(F32)
    pack[...] = pack_f[...].astype(BF16)
    pl.semaphore_wait(barrier, len(peers))

    z_in = [send(pack, near.at[i], near_ss.at[i], near_rs.at[i], at_z(-direct[i])) for i in (1, 3, 0, 2)]

    for copy in copies[2:]:
        copy.wait()
    valid = ep * rows + lax.broadcasted_iota(jnp.int32, (rows, HD), 0) < len_s[x]
    for h in range(heads):
        cols = slice(h * HD, (h + 1) * HD)
        at = slice(h * rows, (h + 1) * rows)
        q_s[at] = q_v[:, cols]
        g_s[at] = jnp.where(valid, g_v[:, cols], jnp.zeros((), BF16))

    z_in[0].wait_recv()
    z_in[2].wait_recv()
    fwd_up = send(near.at[0:2], near.at[4:6], near_ss.at[4], near_rs.at[4], at_z(-far))
    z_in[1].wait_recv()
    z_in[3].wait_recv()
    fwd_down = send(near.at[2:4], near.at[6:8], near_ss.at[5], near_rs.at[5], at_z(far))

    mine = lax.div(z, half)
    per = count // 2

    def plane_gather(part):
        for i in range(part * per, (part + 1) * per):
            packet = near[i].astype(F32)
            if i == count - 1:
                packet = jnp.where(x == 0, pack_f[...], packet)
            packet = jnp.where(mine == 0, packet[: 2 * lanes], packet[2 * lanes :])
            rows_f[0, i * lanes : (i + 1) * lanes] = packet[:lanes]
            rows_f[1, i * lanes : (i + 1) * lanes] = packet[lanes:]
        span_rows = slice(part * part_rows, (part + 1) * part_rows)
        for side in range(2):
            kv[part, 0, 0, 0, side] = rows_f[side, span_rows].astype(BF16)
        return [
            send(
                kv.at[part, 0, 0, 0],
                kv.at[part, 0, oy, ox],
                kv_ss.at[part, oy, ox],
                kv_rs.at[part, oy, ox],
                in_plane(ox, oy),
            )
            for ox, oy in plane
        ]

    def share(part, arriving):
        for copy in reversed(arriving):
            copy.wait_recv()
        return send(kv.at[part, 0], kv.at[part, 1], sib_ss.at[part], sib_rs.at[part], sib)

    def half_of(part, side):
        return kv[part, :, :, :, side].reshape(mid, HD)

    def against(table, operand):
        return lax.dot_general(table, operand, (((1,), (1,)), ((), ())), preferred_element_type=F32)

    half_one = plane_gather(0)
    fwd_up.wait_recv()
    fwd_down.wait_recv()
    half_two = plane_gather(1)
    share_one = share(0, half_one)
    share_one.wait_recv()
    s_f[...] = against(half_of(0, 0), q_s[...])
    dp_f[...] = against(half_of(0, 1), g_s[...])
    share(1, half_two).wait_recv()

    keys_two = half_of(1, 0)
    values_two = half_of(1, 1)
    factor = scale * math.log2(math.e)
    for h in range(heads):
        at = slice(h * rows, (h + 1) * rows)
        s = [s_f[:, at], against(keys_two, q_s[at])]
        top = jnp.maximum(*[jnp.max(v, axis=0, keepdims=True) for v in s])
        e = [jnp.exp2((v - top) * factor) for v in s]
        inverse = 1.0 / sum(jnp.sum(v, axis=0, keepdims=True) for v in e)
        prob = [v * inverse for v in e]
        dp = [dp_f[:, at], against(values_two, g_s[at])]
        delta = sum(jnp.sum(p * d, axis=0, keepdims=True) for p, d in zip(prob, dp))
        for i in range(2):
            block = slice(i * mid, (i + 1) * mid)
            p_t[block, at] = prob[i].astype(BF16)
            ds_t[block, at] = (prob[i] * (dp[i] - delta)).astype(BF16)

    def partial(side, weights, operand):
        total = jnp.dot(weights[...], operand[...], preferred_element_type=F32)
        acc[side] = total.reshape(2, CORES, ny, nx, part_rows, HD)
        return send(acc.at[side, :, 1], acc_rx.at[side], acc_ss.at[side], acc_rs.at[side], sib)

    v_acc = partial(1, p_t, g_s)
    k_acc = partial(0, ds_t, q_s)

    v_acc.wait_recv()
    v_all = acc[1, :, 0] + acc_rx[1]
    for o in range(1, nx):
        one_tx[1, o] = v_all[:, :, o].astype(BF16)
    v_one = [
        send(one_tx.at[1, o], one_rx.at[1, o], one_ss.at[1, o], one_rs.at[1, o], at_x(-o)) for o in range(1, nx)
    ]
    kept[1] = v_all[:, :, 0]
    k_acc.wait_recv()
    k_all = acc[0, :, 0] + acc_rx[0]
    for o in range(1, ny):
        one_tx[0, o] = k_all[:, o].astype(BF16)
    k_one = [
        send(one_tx.at[0, o], one_rx.at[0, o], one_ss.at[0, o], one_rs.at[0, o], at_y(-o)) for o in range(1, ny)
    ]
    kept[0] = k_all[:, 0]

    for copy in v_one:
        copy.wait_recv()
    v_half = kept[1]
    for o in range(1, nx):
        v_half += one_rx[1, o].astype(F32)
    for o in range(ny):
        two_tx[1, o] = v_half[:, o]
    v_two = [
        send(two_tx.at[1, o], two_rx.at[1, o], two_ss.at[1, o], two_rs.at[1, o], at_y(-o)) for o in range(1, ny)
    ]
    for copy in k_one:
        copy.wait_recv()
    k_half = kept[0]
    for o in range(1, ny):
        k_half += one_rx[0, o].astype(F32)
    for o in range(nx):
        two_tx[0, o] = k_half[:, o]
    k_two = [
        send(two_tx.at[0, o], two_rx.at[0, o], two_ss.at[0, o], two_rs.at[0, o], at_x(-o)) for o in range(1, nx)
    ]
    for copy in v_two:
        copy.wait_recv()
    for copy in k_two:
        copy.wait_recv()
    for part, size in ((0, nx), (1, ny)):
        total = two_tx[part, 0]
        for o in range(1, size):
            total += two_rx[part, o]
        rows_f[part] = total.reshape(2 * part_rows, HD)
    for i in range(count):
        for part in range(2):
            z_tx[i, part * lanes : (part + 1) * lanes] = rows_f[part, i * lanes : (i + 1) * lanes]

    def z_copy(i):
        return pltpu.make_async_remote_copy(
            src_ref=z_tx.at[i],
            dst_ref=z_rx.at[i],
            send_sem=z_ss.at[i],
            recv_sem=z_rs.at[i],
            device_id=at_z(offsets[i]),
            device_id_type=MESH,
        )

    for i in (5, 4, 6, 1, 3, 0, 2):
        z_copy(i).start()

    @pl.when(x != 0)
    def _():
        z_copy(count - 1).start()

    @pl.when(x == 0)
    def _():
        z_rx[count - 1] = z_tx[count - 1]

    keys = kv[:, :, :, :, 0].reshape(span, HD)
    gq_t = jnp.dot(keys.T, ds_t[...], preferred_element_type=F32) * scale
    for h in range(heads):
        gq_v[:, h * HD : (h + 1) * HD] = gq_t[:, h * rows : (h + 1) * rows].T
    gq_out = pltpu.make_async_copy(gq_v, gq_hbm.at[0], out_sem.at[0])
    gq_out.start()
    while sent:
        sent.pop().wait_send()

    for i in range(count - 1):
        z_copy(i).wait_recv()

    @pl.when(x != 0)
    def _():
        z_copy(count - 1).wait_recv()

    for h in range(KVH):
        total = jnp.zeros((2 * lanes, HD), F32)
        for i in range(count):
            source = lax.rem(z - offsets[i] + nz, nz)
            total += jnp.where(lax.div(source, half) == h, z_rx[i], 0.0)
        x_tx[h] = total
    last = [send(x_tx, x_rx.at[o], x_ss.at[o], x_rs.at[o], at_x(o)) for o in range(1, nx)]
    for i in range(count - 1):
        z_copy(i).wait_send()

    @pl.when(x != 0)
    def _():
        z_copy(count - 1).wait_send()

    for copy in last:
        copy.wait_recv()
    for h in range(KVH):
        total = x_tx[h]
        for o in range(1, nx):
            total += x_rx[o, h]
        gk_v[:, h * HD : (h + 1) * HD] = total[:lanes] * scale
        gv_v[:, h * HD : (h + 1) * HD] = total[lanes:]
    gk_out = pltpu.make_async_copy(gk_v, gk_hbm, out_sem.at[1])
    gv_out = pltpu.make_async_copy(gv_v, gv_hbm, out_sem.at[2])
    gk_out.start()
    gv_out.start()

    while sent:
        sent.pop().wait_send()
    gq_out.wait()
    gk_out.wait()
    gv_out.wait()


def hand_over(gq, gk, gv, gq_out, gk_out, gv_out):
    gq_out[...] = gq[...]
    gk_out[...] = gk[...]
    gv_out[...] = gv[...]


def make(mesh, ny):
    nx = mesh.shape["resp"]
    zl = mesh.shape["ep"] // ny
    zh = mesh.shape["kv"] // CORES
    geo = (nx, ny, zl, zh)
    count = zl * zh // nx

    def body(lengths, queries, grad_out, prompt_keys, prompt_values):
        rows = queries.shape[1]
        width = queries.shape[2] // mesh.shape["kv"]
        lanes = prompt_keys.shape[0]
        part_rows = count * lanes // 2
        span = CORES * 2 * nx * ny * part_rows
        stacked = rows * width // HD
        side = max(nx, ny)
        dma = pltpu.SemaphoreType.DMA
        hbm = pl.BlockSpec(memory_space=pltpu.HBM)
        out_shape = (
            jax.ShapeDtypeStruct((1, rows, width), F32),
            jax.ShapeDtypeStruct(prompt_keys.shape, F32),
            jax.ShapeDtypeStruct(prompt_values.shape, F32),
        )
        grads = pl.pallas_call(
            functools.partial(kernel, geo),
            out_shape=out_shape,
            in_specs=[hbm] * 5,
            out_specs=(hbm, hbm, hbm),
            scratch_shapes=[
                pltpu.SMEM(lengths.shape, jnp.int32),
                pltpu.VMEM(prompt_keys.shape, BF16),
                pltpu.VMEM(prompt_values.shape, BF16),
                pltpu.VMEM((rows, width), BF16),
                pltpu.VMEM((rows, width), BF16),
                pltpu.VMEM((stacked, HD), BF16),
                pltpu.VMEM((stacked, HD), BF16),
                pltpu.VMEM((4 * lanes, HD), F32),
                pltpu.VMEM((4 * lanes, HD), BF16),
                pltpu.VMEM((count, 4 * lanes, HD), BF16),
                pltpu.VMEM((2, 2 * part_rows, HD), F32),
                pltpu.VMEM((2, CORES, ny, nx, 2, part_rows, HD), BF16),
                pltpu.VMEM((span // 2, stacked), F32),
                pltpu.VMEM((span // 2, stacked), F32),
                pltpu.VMEM((span, stacked), BF16),
                pltpu.VMEM((span, stacked), BF16),
                pltpu.VMEM((2, 2, CORES, ny, nx, part_rows, HD), F32),
                pltpu.VMEM((2, 2, ny, nx, part_rows, HD), F32),
                pltpu.VMEM((2, 2, side, part_rows, HD), F32),
                pltpu.VMEM((2, side, 2, side, part_rows, HD), BF16),
                pltpu.VMEM((2, side, 2, side, part_rows, HD), BF16),
                pltpu.VMEM((2, side, 2, part_rows, HD), F32),
                pltpu.VMEM((2, side, 2, part_rows, HD), F32),
                pltpu.VMEM((count, 2 * lanes, HD), F32),
                pltpu.VMEM((count, 2 * lanes, HD), F32),
                pltpu.VMEM((KVH, 2 * lanes, HD), F32),
                pltpu.VMEM((nx, KVH, 2 * lanes, HD), F32),
                pltpu.VMEM((rows, width), F32),
                pltpu.VMEM(prompt_keys.shape, F32),
                pltpu.VMEM(prompt_values.shape, F32),
                dma((5,)),
                dma((3,)),
                dma((6,)),
                dma((6,)),
                dma((2, ny, nx)),
                dma((2, ny, nx)),
                dma((2,)),
                dma((2,)),
                dma((2,)),
                dma((2,)),
                dma((2, side)),
                dma((2, side)),
                dma((2, side)),
                dma((2, side)),
                dma((count,)),
                dma((count,)),
                dma((nx,)),
                dma((nx,)),
            ],
            compiler_params=pltpu.CompilerParams(
                collective_id=0, has_side_effects=True, vmem_limit_bytes=60 * 1024 * 1024
            ),
        )(lengths, queries, grad_out, prompt_keys, prompt_values)
        return pl.pallas_call(hand_over, out_shape=out_shape)(*grads)

    return jax.shard_map(
        body,
        mesh=mesh,
        in_specs=(
            P(),
            P("resp", "ep", None),
            P("resp", "ep", None),
            P(("ep", "kv"), None),
            P(("ep", "kv"), None),
        ),
        out_specs=(P("resp", "ep", "kv"), P(("ep", "kv"), None), P(("ep", "kv"), None)),
        check_vma=False,
    )


def solution(mesh):
    return make(mesh, NY)
```

```python
import functools
import math

import jax
import jax.numpy as jnp
from jax import lax
from jax.experimental import pallas as pl
from jax.experimental.pallas import tpu as pltpu
from jax.sharding import PartitionSpec as P

HD = 128
KVH = 2
CORES = 2
NY = 4
MESH = pl.DeviceIdType.MESH
BF16 = jnp.bfloat16
F32 = jnp.float32


def kernel(
    geo,
    len_hbm,
    q_hbm,
    g_hbm,
    k_hbm,
    v_hbm,
    gq_hbm,
    gk_hbm,
    gv_hbm,
    len_s,
    k_v,
    v_v,
    q_v,
    g_v,
    q_s,
    g_s,
    pack_f,
    pack,
    near,
    rows_f,
    kv,
    s_f,
    dp_f,
    p_t,
    ds_t,
    acc,
    acc_rx,
    kept,
    one_tx,
    one_rx,
    z_tx,
    z_rx,
    x_tx,
    x_rx,
    gq_v,
    gk_v,
    gv_v,
    in_sem,
    out_sem,
    near_ss,
    near_rs,
    kv_ss,
    kv_rs,
    sib_ss,
    sib_rs,
    acc_ss,
    acc_rs,
    one_ss,
    one_rs,
    z_ss,
    z_rs,
    x_ss,
    x_rs,
):
    nx, ny, zl, zh = geo
    nz = zl * zh
    half = nz // KVH
    far = nz // 4
    rows = q_v.shape[0]
    width = q_v.shape[1]
    heads = width // HD
    lanes = k_v.shape[0]
    part_rows = kv.shape[5]
    span = CORES * 2 * nx * ny * part_rows
    mid = span // 2
    scale = 1.0 / math.sqrt(HD)

    x = lax.axis_index("resp")
    ep = lax.axis_index("ep")
    kvi = lax.axis_index("kv")
    y, z_lo = lax.div(ep, zl), lax.rem(ep, zl)
    z_hi, c = lax.div(kvi, CORES), lax.rem(kvi, CORES)
    z = z_hi * zl + z_lo

    def at_z(offset):
        zz = lax.rem(z + offset + nz, nz)
        return (x, y * zl + lax.rem(zz, zl), lax.div(zz, zl) * CORES + c)

    def at_x(offset):
        return (lax.rem(x + offset + nx, nx), ep, kvi)

    def in_plane(ox, oy):
        return (lax.rem(x + ox + nx, nx), lax.rem(y + oy + ny, ny) * zl + z_lo, kvi)

    sib = (x, ep, z_hi * CORES + 1 - c)

    plane = [(ox, oy) for ox in range(nx) for oy in range(ny) if ox or oy]
    plane.sort(key=lambda o: -min(o[0], nx - o[0]) - min(o[1], ny - o[1]))

    first = jnp.where(x == 0, nx, x)
    second = first + nx
    direct = [first, second, -first, -second]
    relayed = [first + far, second + far, -first - far, jnp.where(x == 0, 0, -second - far)]
    offsets = direct + relayed
    count = len(offsets)

    barrier = pltpu.get_barrier_semaphore()
    peers = [at_z(o) for o in (-far, far, -second, second, -first, first)]
    peers += [in_plane(*o) for o in plane] + [sib]
    for peer in peers:
        pl.semaphore_signal(barrier, inc=1, device_id=peer, device_id_type=MESH)

    copies = [
        pltpu.make_async_copy(k_hbm, k_v, in_sem.at[0]),
        pltpu.make_async_copy(v_hbm, v_v, in_sem.at[1]),
        pltpu.make_async_copy(len_hbm, len_s, in_sem.at[2]),
    ]
    own = pl.ds(pl.multiple_of(kvi * width, width), width)
    copies.append(pltpu.make_async_copy(q_hbm.at[0, :, own], q_v, in_sem.at[3]))
    copies.append(pltpu.make_async_copy(g_hbm.at[0, :, own], g_v, in_sem.at[4]))
    for copy in copies:
        copy.start()

    sent = []

    def send(src, dst, ss, rs, device):
        copy = pltpu.make_async_remote_copy(
            src_ref=src, dst_ref=dst, send_sem=ss, recv_sem=rs, device_id=device, device_id_type=MESH
        )
        copy.start()
        sent.append(copy)
        return copy

    copies[0].wait()
    copies[1].wait()
    for h in range(KVH):
        for part, ref in enumerate((k_v, v_v)):
            at = (2 * h + part) * lanes
            pack_f[at : at + lanes] = ref[:, h * HD : (h + 1) * HD].astype(F32)
    pack[...] = pack_f[...].astype(BF16)
    pl.semaphore_wait(barrier, len(peers))

    z_in = [send(pack, near.at[i], near_ss.at[i], near_rs.at[i], at_z(-direct[i])) for i in (1, 3, 0, 2)]

    for copy in copies[2:]:
        copy.wait()
    valid = ep * rows + lax.broadcasted_iota(jnp.int32, (rows, HD), 0) < len_s[x]
    for h in range(heads):
        cols = slice(h * HD, (h + 1) * HD)
        at = slice(h * rows, (h + 1) * rows)
        q_s[at] = q_v[:, cols]
        g_s[at] = jnp.where(valid, g_v[:, cols], jnp.zeros((), BF16))

    z_in[0].wait_recv()
    z_in[2].wait_recv()
    fwd_up = send(near.at[0:2], near.at[4:6], near_ss.at[4], near_rs.at[4], at_z(-far))
    z_in[1].wait_recv()
    z_in[3].wait_recv()
    fwd_down = send(near.at[2:4], near.at[6:8], near_ss.at[5], near_rs.at[5], at_z(far))

    mine = lax.div(z, half)
    per = count // 2

    def plane_gather(part):
        for i in range(part * per, (part + 1) * per):
            packet = near[i].astype(F32)
            if i == count - 1:
                packet = jnp.where(x == 0, pack_f[...], packet)
            packet = jnp.where(mine == 0, packet[: 2 * lanes], packet[2 * lanes :])
            rows_f[0, i * lanes : (i + 1) * lanes] = packet[:lanes]
            rows_f[1, i * lanes : (i + 1) * lanes] = packet[lanes:]
        span_rows = slice(part * part_rows, (part + 1) * part_rows)
        for side in range(2):
            kv[part, 0, 0, 0, side] = rows_f[side, span_rows].astype(BF16)
        return [
            send(
                kv.at[part, 0, 0, 0],
                kv.at[part, 0, oy, ox],
                kv_ss.at[part, oy, ox],
                kv_rs.at[part, oy, ox],
                in_plane(ox, oy),
            )
            for ox, oy in plane
        ]

    def share(part, arriving):
        for copy in reversed(arriving):
            copy.wait_recv()
        return send(kv.at[part, 0], kv.at[part, 1], sib_ss.at[part], sib_rs.at[part], sib)

    def half_of(part, side):
        return kv[part, :, :, :, side].reshape(mid, HD)

    def against(table, operand):
        return lax.dot_general(table, operand, (((1,), (1,)), ((), ())), preferred_element_type=F32)

    half_one = plane_gather(0)
    fwd_up.wait_recv()
    fwd_down.wait_recv()
    half_two = plane_gather(1)
    share_one = share(0, half_one)
    share_one.wait_recv()
    s_f[...] = against(half_of(0, 0), q_s[...])
    dp_f[...] = against(half_of(0, 1), g_s[...])
    share(1, half_two).wait_recv()

    keys_two = half_of(1, 0)
    values_two = half_of(1, 1)
    factor = scale * math.log2(math.e)
    for h in range(heads):
        at = slice(h * rows, (h + 1) * rows)
        s = [s_f[:, at], against(keys_two, q_s[at])]
        top = jnp.maximum(*[jnp.max(v, axis=0, keepdims=True) for v in s])
        e = [jnp.exp2((v - top) * factor) for v in s]
        inverse = 1.0 / sum(jnp.sum(v, axis=0, keepdims=True) for v in e)
        prob = [v * inverse for v in e]
        dp = [dp_f[:, at], against(values_two, g_s[at])]
        delta = sum(jnp.sum(p * d, axis=0, keepdims=True) for p, d in zip(prob, dp))
        for i in range(2):
            block = slice(i * mid, (i + 1) * mid)
            p_t[block, at] = prob[i].astype(BF16)
            ds_t[block, at] = (prob[i] * (dp[i] - delta)).astype(BF16)

    def partial(side, weights, operand):
        total = jnp.dot(weights[...], operand[...], preferred_element_type=F32)
        acc[side] = total.reshape(2, CORES, ny, nx, part_rows, HD)
        return send(acc.at[side, :, 1], acc_rx.at[side], acc_ss.at[side], acc_rs.at[side], sib)

    v_acc = partial(1, p_t, g_s)
    k_acc = partial(0, ds_t, q_s)

    def scatter(side, copy):
        copy.wait_recv()
        both = acc[side, :, 0] + acc_rx[side]
        kept[side] = both[:, 0, 0]
        for ox, oy in plane:
            one_tx[side, oy, ox] = both[:, oy, ox].astype(BF16)
        return [
            send(
                one_tx.at[side, oy, ox],
                one_rx.at[side, oy, ox],
                one_ss.at[side, oy, ox],
                one_rs.at[side, oy, ox],
                in_plane(-ox, -oy),
            )
            for ox, oy in plane
        ]

    def collect(side, arriving):
        total = kept[side]
        for copy, (ox, oy) in reversed(list(zip(arriving, plane))):
            copy.wait_recv()
            total += one_rx[side, oy, ox].astype(F32)
        rows_f[side] = total.reshape(2 * part_rows, HD)

    v_one = scatter(1, v_acc)
    k_one = scatter(0, k_acc)
    collect(1, v_one)
    collect(0, k_one)
    for i in range(count):
        for part in range(2):
            z_tx[i, part * lanes : (part + 1) * lanes] = rows_f[part, i * lanes : (i + 1) * lanes]

    def z_copy(i):
        return pltpu.make_async_remote_copy(
            src_ref=z_tx.at[i],
            dst_ref=z_rx.at[i],
            send_sem=z_ss.at[i],
            recv_sem=z_rs.at[i],
            device_id=at_z(offsets[i]),
            device_id_type=MESH,
        )

    for i in (5, 4, 6, 1, 3, 0, 2):
        z_copy(i).start()

    @pl.when(x != 0)
    def _():
        z_copy(count - 1).start()

    @pl.when(x == 0)
    def _():
        z_rx[count - 1] = z_tx[count - 1]

    keys = kv[:, :, :, :, 0].reshape(span, HD)
    gq_t = jnp.dot(keys.T, ds_t[...], preferred_element_type=F32) * scale
    for h in range(heads):
        gq_v[:, h * HD : (h + 1) * HD] = gq_t[:, h * rows : (h + 1) * rows].T
    gq_out = pltpu.make_async_copy(gq_v, gq_hbm.at[0], out_sem.at[0])
    gq_out.start()
    while sent:
        sent.pop().wait_send()

    for i in range(count - 1):
        z_copy(i).wait_recv()

    @pl.when(x != 0)
    def _():
        z_copy(count - 1).wait_recv()

    for h in range(KVH):
        total = jnp.zeros((2 * lanes, HD), F32)
        for i in range(count):
            source = lax.rem(z - offsets[i] + nz, nz)
            total += jnp.where(lax.div(source, half) == h, z_rx[i], 0.0)
        x_tx[h] = total
    last = [send(x_tx, x_rx.at[o], x_ss.at[o], x_rs.at[o], at_x(o)) for o in range(1, nx)]
    for i in range(count - 1):
        z_copy(i).wait_send()

    @pl.when(x != 0)
    def _():
        z_copy(count - 1).wait_send()

    for copy in last:
        copy.wait_recv()
    for h in range(KVH):
        total = x_tx[h]
        for o in range(1, nx):
            total += x_rx[o, h]
        gk_v[:, h * HD : (h + 1) * HD] = total[:lanes] * scale
        gv_v[:, h * HD : (h + 1) * HD] = total[lanes:]
    gk_out = pltpu.make_async_copy(gk_v, gk_hbm, out_sem.at[1])
    gv_out = pltpu.make_async_copy(gv_v, gv_hbm, out_sem.at[2])
    gk_out.start()
    gv_out.start()

    while sent:
        sent.pop().wait_send()
    gq_out.wait()
    gk_out.wait()
    gv_out.wait()


def hand_over(gq, gk, gv, gq_out, gk_out, gv_out):
    gq_out[...] = gq[...]
    gk_out[...] = gk[...]
    gv_out[...] = gv[...]


def make(mesh, ny):
    nx = mesh.shape["resp"]
    zl = mesh.shape["ep"] // ny
    zh = mesh.shape["kv"] // CORES
    geo = (nx, ny, zl, zh)
    count = zl * zh // nx

    def body(lengths, queries, grad_out, prompt_keys, prompt_values):
        rows = queries.shape[1]
        width = queries.shape[2] // mesh.shape["kv"]
        lanes = prompt_keys.shape[0]
        part_rows = count * lanes // 2
        span = CORES * 2 * nx * ny * part_rows
        stacked = rows * width // HD
        dma = pltpu.SemaphoreType.DMA
        hbm = pl.BlockSpec(memory_space=pltpu.HBM)
        out_shape = (
            jax.ShapeDtypeStruct((1, rows, width), F32),
            jax.ShapeDtypeStruct(prompt_keys.shape, F32),
            jax.ShapeDtypeStruct(prompt_values.shape, F32),
        )
        grads = pl.pallas_call(
            functools.partial(kernel, geo),
            out_shape=out_shape,
            in_specs=[hbm] * 5,
            out_specs=(hbm, hbm, hbm),
            scratch_shapes=[
                pltpu.SMEM(lengths.shape, jnp.int32),
                pltpu.VMEM(prompt_keys.shape, BF16),
                pltpu.VMEM(prompt_values.shape, BF16),
                pltpu.VMEM((rows, width), BF16),
                pltpu.VMEM((rows, width), BF16),
                pltpu.VMEM((stacked, HD), BF16),
                pltpu.VMEM((stacked, HD), BF16),
                pltpu.VMEM((4 * lanes, HD), F32),
                pltpu.VMEM((4 * lanes, HD), BF16),
                pltpu.VMEM((count, 4 * lanes, HD), BF16),
                pltpu.VMEM((2, 2 * part_rows, HD), F32),
                pltpu.VMEM((2, CORES, ny, nx, 2, part_rows, HD), BF16),
                pltpu.VMEM((span // 2, stacked), F32),
                pltpu.VMEM((span // 2, stacked), F32),
                pltpu.VMEM((span, stacked), BF16),
                pltpu.VMEM((span, stacked), BF16),
                pltpu.VMEM((2, 2, CORES, ny, nx, part_rows, HD), F32),
                pltpu.VMEM((2, 2, ny, nx, part_rows, HD), F32),
                pltpu.VMEM((2, 2, part_rows, HD), F32),
                pltpu.VMEM((2, ny, nx, 2, part_rows, HD), BF16),
                pltpu.VMEM((2, ny, nx, 2, part_rows, HD), BF16),
                pltpu.VMEM((count, 2 * lanes, HD), F32),
                pltpu.VMEM((count, 2 * lanes, HD), F32),
                pltpu.VMEM((KVH, 2 * lanes, HD), F32),
                pltpu.VMEM((nx, KVH, 2 * lanes, HD), F32),
                pltpu.VMEM((rows, width), F32),
                pltpu.VMEM(prompt_keys.shape, F32),
                pltpu.VMEM(prompt_values.shape, F32),
                dma((5,)),
                dma((3,)),
                dma((6,)),
                dma((6,)),
                dma((2, ny, nx)),
                dma((2, ny, nx)),
                dma((2,)),
                dma((2,)),
                dma((2,)),
                dma((2,)),
                dma((2, ny, nx)),
                dma((2, ny, nx)),
                dma((count,)),
                dma((count,)),
                dma((nx,)),
                dma((nx,)),
            ],
            compiler_params=pltpu.CompilerParams(
                collective_id=0, has_side_effects=True, vmem_limit_bytes=60 * 1024 * 1024
            ),
        )(lengths, queries, grad_out, prompt_keys, prompt_values)
        return pl.pallas_call(hand_over, out_shape=out_shape)(*grads)

    return jax.shard_map(
        body,
        mesh=mesh,
        in_specs=(
            P(),
            P("resp", "ep", None),
            P("resp", "ep", None),
            P(("ep", "kv"), None),
            P(("ep", "kv"), None),
        ),
        out_specs=(P("resp", "ep", "kv"), P(("ep", "kv"), None), P(("ep", "kv"), None)),
        check_vma=False,
    )


def solution(mesh):
    return make(mesh, NY)
```

```python
import functools
import math

import jax
import jax.numpy as jnp
from jax import lax
from jax.experimental import pallas as pl
from jax.experimental.pallas import tpu as pltpu
from jax.sharding import PartitionSpec as P

HD = 128
KVH = 2
CORES = 2
NY = 4
MESH = pl.DeviceIdType.MESH
BF16 = jnp.bfloat16
F32 = jnp.float32


def kernel(
    geo,
    len_hbm,
    q_hbm,
    g_hbm,
    k_hbm,
    v_hbm,
    gq_hbm,
    gk_hbm,
    gv_hbm,
    len_s,
    k_v,
    v_v,
    q_v,
    g_v,
    q_s,
    g_s,
    pack_f,
    pack,
    near,
    rows_f,
    kv,
    e_f,
    dp_f,
    st_half,
    st_tx,
    st_rx,
    p_t,
    ds_t,
    acc,
    one_tx,
    one_rx,
    z_tx,
    z_rx,
    x_tx,
    x_rx,
    gq_p,
    gq_rx,
    gq_v,
    gk_v,
    gv_v,
    in_sem,
    out_sem,
    near_ss,
    near_rs,
    kv_ss,
    kv_rs,
    st_ss,
    st_rs,
    gq_ss,
    gq_rs,
    one_ss,
    one_rs,
    z_ss,
    z_rs,
    x_ss,
    x_rs,
):
    nx, ny, zl, zh = geo
    nz = zl * zh
    half = nz // KVH
    far = nz // 4
    rows = q_v.shape[0]
    width = q_v.shape[1]
    heads = width // HD
    lanes = k_v.shape[0]
    part_rows = kv.shape[4]
    span = 2 * nx * ny * part_rows
    mid = span // 2
    scale = 1.0 / math.sqrt(HD)

    x = lax.axis_index("resp")
    ep = lax.axis_index("ep")
    kvi = lax.axis_index("kv")
    y, z_lo = lax.div(ep, zl), lax.rem(ep, zl)
    z_hi, c = lax.div(kvi, CORES), lax.rem(kvi, CORES)
    z = z_hi * zl + z_lo

    def at_z(offset):
        zz = lax.rem(z + offset + nz, nz)
        return (x, y * zl + lax.rem(zz, zl), lax.div(zz, zl) * CORES + c)

    def at_x(offset):
        return (lax.rem(x + offset + nx, nx), ep, kvi)

    def in_plane(ox, oy):
        return (lax.rem(x + ox + nx, nx), lax.rem(y + oy + ny, ny) * zl + z_lo, kvi)

    sib = (x, ep, z_hi * CORES + 1 - c)

    plane = [(ox, oy) for ox in range(nx) for oy in range(ny) if ox or oy]
    plane.sort(key=lambda o: -min(o[0], nx - o[0]) - min(o[1], ny - o[1]))

    first = jnp.where(x == 0, nx, x)
    second = first + nx
    direct = [first, second, -first, -second]
    relayed = [first + far, second + far, -first - far, jnp.where(x == 0, 0, -second - far)]
    offsets = direct + relayed
    count = len(offsets)

    barrier = pltpu.get_barrier_semaphore()
    peers = [at_z(o) for o in (-far, far, -second, second, -first, first)]
    peers += [in_plane(*o) for o in plane] + [sib]
    for peer in peers:
        pl.semaphore_signal(barrier, inc=1, device_id=peer, device_id_type=MESH)

    copies = [
        pltpu.make_async_copy(k_hbm, k_v, in_sem.at[0]),
        pltpu.make_async_copy(v_hbm, v_v, in_sem.at[1]),
        pltpu.make_async_copy(len_hbm, len_s, in_sem.at[2]),
    ]
    own = pl.ds(pl.multiple_of(z_hi * width, width), width)
    copies.append(pltpu.make_async_copy(q_hbm.at[0, :, own], q_v, in_sem.at[3]))
    copies.append(pltpu.make_async_copy(g_hbm.at[0, :, own], g_v, in_sem.at[4]))
    for copy in copies:
        copy.start()

    sent = []

    def send(src, dst, ss, rs, device):
        copy = pltpu.make_async_remote_copy(
            src_ref=src, dst_ref=dst, send_sem=ss, recv_sem=rs, device_id=device, device_id_type=MESH
        )
        copy.start()
        sent.append(copy)
        return copy

    copies[0].wait()
    copies[1].wait()
    for h in range(KVH):
        for part, ref in enumerate((k_v, v_v)):
            at = (2 * h + part) * lanes
            pack_f[at : at + lanes] = ref[:, h * HD : (h + 1) * HD].astype(F32)
    pack[...] = pack_f[...].astype(BF16)
    pl.semaphore_wait(barrier, len(peers))

    z_in = [send(pack, near.at[i], near_ss.at[i], near_rs.at[i], at_z(-direct[i])) for i in (1, 3, 0, 2)]

    for copy in copies[2:]:
        copy.wait()
    valid = ep * rows + lax.broadcasted_iota(jnp.int32, (rows, HD), 0) < len_s[x]
    for h in range(heads):
        cols = slice(h * HD, (h + 1) * HD)
        at = slice(h * rows, (h + 1) * rows)
        q_s[at] = q_v[:, cols]
        g_s[at] = jnp.where(valid, g_v[:, cols], jnp.zeros((), BF16))

    z_in[0].wait_recv()
    z_in[2].wait_recv()
    fwd_up = send(near.at[0:2], near.at[4:6], near_ss.at[4], near_rs.at[4], at_z(-far))
    z_in[1].wait_recv()
    z_in[3].wait_recv()
    fwd_down = send(near.at[2:4], near.at[6:8], near_ss.at[5], near_rs.at[5], at_z(far))

    mine = lax.div(z, half)
    per = count // 2

    def plane_gather(part):
        for i in range(part * per, (part + 1) * per):
            packet = near[i].astype(F32)
            if i == count - 1:
                packet = jnp.where(x == 0, pack_f[...], packet)
            packet = jnp.where(mine == 0, packet[: 2 * lanes], packet[2 * lanes :])
            rows_f[0, i * lanes : (i + 1) * lanes] = packet[:lanes]
            rows_f[1, i * lanes : (i + 1) * lanes] = packet[lanes:]
        span_rows = slice(part * part_rows, (part + 1) * part_rows)
        for side in range(2):
            kv[part, 0, 0, side] = rows_f[side, span_rows].astype(BF16)
        return [
            send(
                kv.at[part, 0, 0],
                kv.at[part, oy, ox],
                kv_ss.at[part, oy, ox],
                kv_rs.at[part, oy, ox],
                in_plane(ox, oy),
            )
            for ox, oy in plane
        ]

    def half_of(part, side):
        return kv[part, :, :, side].reshape(mid, HD)

    def against(table, operand):
        return lax.dot_general(table, operand, (((1,), (1,)), ((), ())), preferred_element_type=F32)

    half_one = plane_gather(0)
    fwd_up.wait_recv()
    fwd_down.wait_recv()
    half_two = plane_gather(1)
    factor = scale * math.log2(math.e)

    def first_pass(part, arriving):
        for copy in reversed(arriving):
            copy.wait_recv()
        block = slice(part * mid, (part + 1) * mid)
        keys, values = half_of(part, 0), half_of(part, 1)
        for h in range(heads):
            at = slice(h * rows, (h + 1) * rows)
            s = against(keys, q_s[at])
            dp = against(values, g_s[at])
            top = jnp.max(s, axis=0, keepdims=True)
            e = jnp.exp2((s - top) * factor)
            e_f[block, at] = e
            dp_f[block, at] = dp
            st_half[part, 0, h : h + 1, :rows] = top
            st_half[part, 1, h : h + 1, :rows] = jnp.sum(e, axis=0, keepdims=True)
            st_half[part, 2, h : h + 1, :rows] = jnp.sum(e * dp, axis=0, keepdims=True)

    first_pass(0, half_one)
    first_pass(1, half_two)

    def joined(stats):
        joint = jnp.maximum(stats[0][0], stats[1][0])
        weights = [jnp.exp2((stat[0] - joint) * factor) for stat in stats]
        return [joint] + [sum(stat[k] * w for stat, w in zip(stats, weights)) for k in (1, 2)]

    st_tx[0], st_tx[1], st_tx[2] = joined([st_half[0], st_half[1]])
    send(st_tx, st_rx, st_ss, st_rs, sib).wait_recv()
    joint, total, inner = joined([st_tx[...], st_rx[...]])
    inverse = 1.0 / total
    delta = inner * inverse
    for part in range(2):
        block = slice(part * mid, (part + 1) * mid)
        weight = jnp.exp2((st_half[part, 0] - joint) * factor) * inverse
        for h in range(heads):
            at = slice(h * rows, (h + 1) * rows)
            prob = e_f[block, at] * weight[h : h + 1, :rows]
            p_t[block, at] = prob.astype(BF16)
            ds_t[block, at] = (prob * (dp_f[block, at] - delta[h : h + 1, :rows])).astype(BF16)

    for side, weights, operand in ((0, ds_t, q_s), (1, p_t, g_s)):
        part_sum = jnp.dot(weights[...], operand[...], preferred_element_type=F32)
        part_sum = part_sum.reshape(2, ny, nx, part_rows, HD)
        acc[side] = part_sum[:, 0, 0]
        for ox, oy in plane:
            one_tx[oy, ox, side] = part_sum[:, oy, ox].astype(BF16)
    arriving = [
        send(one_tx.at[oy, ox], one_rx.at[oy, ox], one_ss.at[oy, ox], one_rs.at[oy, ox], in_plane(-ox, -oy))
        for ox, oy in plane
    ]
    plane_sum = acc[...]
    for copy, (ox, oy) in reversed(list(zip(arriving, plane))):
        copy.wait_recv()
        plane_sum += one_rx[oy, ox].astype(F32)
    rows_f[...] = plane_sum.reshape(2, 2 * part_rows, HD)
    for i in range(count):
        for part in range(2):
            z_tx[i, part * lanes : (part + 1) * lanes] = rows_f[part, i * lanes : (i + 1) * lanes]

    def z_copy(i):
        return pltpu.make_async_remote_copy(
            src_ref=z_tx.at[i],
            dst_ref=z_rx.at[i],
            send_sem=z_ss.at[i],
            recv_sem=z_rs.at[i],
            device_id=at_z(offsets[i]),
            device_id_type=MESH,
        )

    for i in (5, 4, 6, 1, 3, 0, 2):
        z_copy(i).start()

    @pl.when(x != 0)
    def _():
        z_copy(count - 1).start()

    @pl.when(x == 0)
    def _():
        z_rx[count - 1] = z_tx[count - 1]

    keys_t = kv[:, :, :, 0].reshape(span, HD).T
    own_cols = heads // CORES * rows
    for core in range(CORES):
        block = slice(core * own_cols, (core + 1) * own_cols)
        gq_p[core] = jnp.dot(keys_t, ds_t[:, block], preferred_element_type=F32)
    send(gq_p.at[1 - c], gq_rx, gq_ss, gq_rs, sib).wait_recv()
    gq_t = (gq_p[c] + gq_rx[...]) * scale
    for h in range(heads // CORES):
        gq_v[:, h * HD : (h + 1) * HD] = gq_t[:, h * rows : (h + 1) * rows].T
    gq_out = pltpu.make_async_copy(gq_v, gq_hbm.at[0], out_sem.at[0])
    gq_out.start()
    while sent:
        sent.pop().wait_send()

    for i in range(count - 1):
        z_copy(i).wait_recv()

    @pl.when(x != 0)
    def _():
        z_copy(count - 1).wait_recv()

    for h in range(KVH):
        total = jnp.zeros((2 * lanes, HD), F32)
        for i in range(count):
            source = lax.rem(z - offsets[i] + nz, nz)
            total += jnp.where(lax.div(source, half) == h, z_rx[i], 0.0)
        x_tx[h] = total
    last = [send(x_tx, x_rx.at[o], x_ss.at[o], x_rs.at[o], at_x(o)) for o in range(1, nx)]
    for i in range(count - 1):
        z_copy(i).wait_send()

    @pl.when(x != 0)
    def _():
        z_copy(count - 1).wait_send()

    for copy in last:
        copy.wait_recv()
    for h in range(KVH):
        total = x_tx[h]
        for o in range(1, nx):
            total += x_rx[o, h]
        gk_v[:, h * HD : (h + 1) * HD] = total[:lanes] * scale
        gv_v[:, h * HD : (h + 1) * HD] = total[lanes:]
    gk_out = pltpu.make_async_copy(gk_v, gk_hbm, out_sem.at[1])
    gv_out = pltpu.make_async_copy(gv_v, gv_hbm, out_sem.at[2])
    gk_out.start()
    gv_out.start()

    while sent:
        sent.pop().wait_send()
    gq_out.wait()
    gk_out.wait()
    gv_out.wait()


def hand_over(gq, gk, gv, gq_out, gk_out, gv_out):
    gq_out[...] = gq[...]
    gk_out[...] = gk[...]
    gv_out[...] = gv[...]


def make(mesh, ny):
    nx = mesh.shape["resp"]
    zl = mesh.shape["ep"] // ny
    zh = mesh.shape["kv"] // CORES
    geo = (nx, ny, zl, zh)
    count = zl * zh // nx

    def body(lengths, queries, grad_out, prompt_keys, prompt_values):
        rows = queries.shape[1]
        width = queries.shape[2] // mesh.shape["kv"]
        lanes = prompt_keys.shape[0]
        part_rows = count * lanes // 2
        span = 2 * nx * ny * part_rows
        both = CORES * width
        heads = both // HD
        stacked = rows * heads
        dma = pltpu.SemaphoreType.DMA
        hbm = pl.BlockSpec(memory_space=pltpu.HBM)
        out_shape = (
            jax.ShapeDtypeStruct((1, rows, width), F32),
            jax.ShapeDtypeStruct(prompt_keys.shape, F32),
            jax.ShapeDtypeStruct(prompt_values.shape, F32),
        )
        grads = pl.pallas_call(
            functools.partial(kernel, geo),
            out_shape=out_shape,
            in_specs=[hbm] * 5,
            out_specs=(hbm, hbm, hbm),
            scratch_shapes=[
                pltpu.SMEM(lengths.shape, jnp.int32),
                pltpu.VMEM(prompt_keys.shape, BF16),
                pltpu.VMEM(prompt_values.shape, BF16),
                pltpu.VMEM((rows, both), BF16),
                pltpu.VMEM((rows, both), BF16),
                pltpu.VMEM((stacked, HD), BF16),
                pltpu.VMEM((stacked, HD), BF16),
                pltpu.VMEM((4 * lanes, HD), F32),
                pltpu.VMEM((4 * lanes, HD), BF16),
                pltpu.VMEM((count, 4 * lanes, HD), BF16),
                pltpu.VMEM((2, 2 * part_rows, HD), F32),
                pltpu.VMEM((2, ny, nx, 2, part_rows, HD), BF16),
                pltpu.VMEM((span, stacked), F32),
                pltpu.VMEM((span, stacked), F32),
                pltpu.VMEM((2, 3, heads, HD), F32),
                pltpu.VMEM((3, heads, HD), F32),
                pltpu.VMEM((3, heads, HD), F32),
                pltpu.VMEM((span, stacked), BF16),
                pltpu.VMEM((span, stacked), BF16),
                pltpu.VMEM((2, 2, part_rows, HD), F32),
                pltpu.VMEM((ny, nx, 2, 2, part_rows, HD), BF16),
                pltpu.VMEM((ny, nx, 2, 2, part_rows, HD), BF16),
                pltpu.VMEM((count, 2 * lanes, HD), F32),
                pltpu.VMEM((count, 2 * lanes, HD), F32),
                pltpu.VMEM((KVH, 2 * lanes, HD), F32),
                pltpu.VMEM((nx, KVH, 2 * lanes, HD), F32),
                pltpu.VMEM((CORES, HD, stacked // CORES), F32),
                pltpu.VMEM((HD, stacked // CORES), F32),
                pltpu.VMEM((rows, width), F32),
                pltpu.VMEM(prompt_keys.shape, F32),
                pltpu.VMEM(prompt_values.shape, F32),
                dma((5,)),
                dma((3,)),
                dma((6,)),
                dma((6,)),
                dma((2, ny, nx)),
                dma((2, ny, nx)),
                dma,
                dma,
                dma,
                dma,
                dma((ny, nx)),
                dma((ny, nx)),
                dma((count,)),
                dma((count,)),
                dma((nx,)),
                dma((nx,)),
            ],
            compiler_params=pltpu.CompilerParams(
                collective_id=0, has_side_effects=True, vmem_limit_bytes=60 * 1024 * 1024
            ),
        )(lengths, queries, grad_out, prompt_keys, prompt_values)
        return pl.pallas_call(hand_over, out_shape=out_shape)(*grads)

    return jax.shard_map(
        body,
        mesh=mesh,
        in_specs=(
            P(),
            P("resp", "ep", None),
            P("resp", "ep", None),
            P(("ep", "kv"), None),
            P(("ep", "kv"), None),
        ),
        out_specs=(P("resp", "ep", "kv"), P(("ep", "kv"), None), P(("ep", "kv"), None)),
        check_vma=False,
    )


def solution(mesh):
    return make(mesh, NY)
```

```python
import functools
import math

import jax
import jax.numpy as jnp
from jax import lax
from jax.experimental import pallas as pl
from jax.experimental.pallas import tpu as pltpu
from jax.sharding import PartitionSpec as P

HD = 128
KVH = 2
CORES = 2
NY = 4
MESH = pl.DeviceIdType.MESH
BF16 = jnp.bfloat16
F32 = jnp.float32


def kernel(
    geo,
    len_hbm,
    q_hbm,
    g_hbm,
    k_hbm,
    v_hbm,
    gq_ref,
    gk_ref,
    gv_ref,
    len_s,
    k_v,
    v_v,
    q_v,
    g_v,
    q_s,
    g_s,
    pack_f,
    pack,
    near,
    rows_f,
    kv,
    e_f,
    dp_f,
    st_half,
    st_tx,
    st_rx,
    p_t,
    ds_t,
    acc,
    one_tx,
    one_rx,
    z_tx,
    z_rx,
    x_tx,
    x_rx,
    gq_p,
    gq_rx,
    in_sem,
    near_ss,
    near_rs,
    kv_ss,
    kv_rs,
    st_ss,
    st_rs,
    gq_ss,
    gq_rs,
    one_ss,
    one_rs,
    z_ss,
    z_rs,
    x_ss,
    x_rs,
):
    nx, ny, zl, zh = geo
    nz = zl * zh
    half = nz // KVH
    far = nz // 4
    rows = q_v.shape[0]
    width = q_v.shape[1]
    heads = width // HD
    lanes = k_v.shape[0]
    part_rows = kv.shape[4]
    span = 2 * nx * ny * part_rows
    mid = span // 2
    scale = 1.0 / math.sqrt(HD)

    x = lax.axis_index("resp")
    ep = lax.axis_index("ep")
    kvi = lax.axis_index("kv")
    y, z_lo = lax.div(ep, zl), lax.rem(ep, zl)
    z_hi, c = lax.div(kvi, CORES), lax.rem(kvi, CORES)
    z = z_hi * zl + z_lo

    def at_z(offset):
        zz = lax.rem(z + offset + nz, nz)
        return (x, y * zl + lax.rem(zz, zl), lax.div(zz, zl) * CORES + c)

    def at_x(offset):
        return (lax.rem(x + offset + nx, nx), ep, kvi)

    def in_plane(ox, oy):
        return (lax.rem(x + ox + nx, nx), lax.rem(y + oy + ny, ny) * zl + z_lo, kvi)

    sib = (x, ep, z_hi * CORES + 1 - c)

    plane = [(ox, oy) for ox in range(nx) for oy in range(ny) if ox or oy]
    plane.sort(key=lambda o: -min(o[0], nx - o[0]) - min(o[1], ny - o[1]))

    first = jnp.where(x == 0, nx, x)
    second = first + nx
    direct = [first, second, -first, -second]
    relayed = [first + far, second + far, -first - far, jnp.where(x == 0, 0, -second - far)]
    offsets = direct + relayed
    count = len(offsets)

    barrier = pltpu.get_barrier_semaphore()
    peers = [at_z(o) for o in (-far, far, -second, second, -first, first)]
    peers += [in_plane(*o) for o in plane] + [sib]
    for peer in peers:
        pl.semaphore_signal(barrier, inc=1, device_id=peer, device_id_type=MESH)

    copies = [
        pltpu.make_async_copy(k_hbm, k_v, in_sem.at[0]),
        pltpu.make_async_copy(v_hbm, v_v, in_sem.at[1]),
        pltpu.make_async_copy(len_hbm, len_s, in_sem.at[2]),
    ]
    own = pl.ds(pl.multiple_of(z_hi * width, width), width)
    copies.append(pltpu.make_async_copy(q_hbm.at[0, :, own], q_v, in_sem.at[3]))
    copies.append(pltpu.make_async_copy(g_hbm.at[0, :, own], g_v, in_sem.at[4]))
    for copy in copies:
        copy.start()

    sent = []

    def send(src, dst, ss, rs, device):
        copy = pltpu.make_async_remote_copy(
            src_ref=src, dst_ref=dst, send_sem=ss, recv_sem=rs, device_id=device, device_id_type=MESH
        )
        copy.start()
        sent.append(copy)
        return copy

    copies[0].wait()
    copies[1].wait()
    for h in range(KVH):
        for part, ref in enumerate((k_v, v_v)):
            at = (2 * h + part) * lanes
            pack_f[at : at + lanes] = ref[:, h * HD : (h + 1) * HD].astype(F32)
    pack[...] = pack_f[...].astype(BF16)
    pl.semaphore_wait(barrier, len(peers))

    z_in = [send(pack, near.at[i], near_ss.at[i], near_rs.at[i], at_z(-direct[i])) for i in (1, 3, 0, 2)]

    for copy in copies[2:]:
        copy.wait()
    valid = ep * rows + lax.broadcasted_iota(jnp.int32, (rows, HD), 0) < len_s[x]
    for h in range(heads):
        cols = slice(h * HD, (h + 1) * HD)
        at = slice(h * rows, (h + 1) * rows)
        q_s[at] = q_v[:, cols]
        g_s[at] = jnp.where(valid, g_v[:, cols], jnp.zeros((), BF16))

    z_in[0].wait_recv()
    z_in[2].wait_recv()
    fwd_up = send(near.at[0:2], near.at[4:6], near_ss.at[4], near_rs.at[4], at_z(-far))
    z_in[1].wait_recv()
    z_in[3].wait_recv()
    fwd_down = send(near.at[2:4], near.at[6:8], near_ss.at[5], near_rs.at[5], at_z(far))

    mine = lax.div(z, half)
    per = count // 2

    def plane_gather(part):
        for i in range(part * per, (part + 1) * per):
            packet = near[i].astype(F32)
            if i == count - 1:
                packet = jnp.where(x == 0, pack_f[...], packet)
            packet = jnp.where(mine == 0, packet[: 2 * lanes], packet[2 * lanes :])
            rows_f[0, i * lanes : (i + 1) * lanes] = packet[:lanes]
            rows_f[1, i * lanes : (i + 1) * lanes] = packet[lanes:]
        span_rows = slice(part * part_rows, (part + 1) * part_rows)
        for side in range(2):
            kv[part, 0, 0, side] = rows_f[side, span_rows].astype(BF16)
        return [
            send(
                kv.at[part, 0, 0],
                kv.at[part, oy, ox],
                kv_ss.at[part, oy, ox],
                kv_rs.at[part, oy, ox],
                in_plane(ox, oy),
            )
            for ox, oy in plane
        ]

    def half_of(part, side):
        return kv[part, :, :, side].reshape(mid, HD)

    def against(table, operand):
        return lax.dot_general(table, operand, (((1,), (1,)), ((), ())), preferred_element_type=F32)

    half_one = plane_gather(0)
    fwd_up.wait_recv()
    fwd_down.wait_recv()
    half_two = plane_gather(1)
    factor = scale * math.log2(math.e)

    def first_pass(part, arriving):
        for copy in reversed(arriving):
            copy.wait_recv()
        block = slice(part * mid, (part + 1) * mid)
        keys, values = half_of(part, 0), half_of(part, 1)
        for h in range(heads):
            at = slice(h * rows, (h + 1) * rows)
            s = against(keys, q_s[at])
            dp = against(values, g_s[at])
            top = jnp.max(s, axis=0, keepdims=True)
            e = jnp.exp2((s - top) * factor)
            e_f[block, at] = e
            dp_f[block, at] = dp
            st_half[part, 0, h : h + 1, :rows] = top
            st_half[part, 1, h : h + 1, :rows] = jnp.sum(e, axis=0, keepdims=True)
            st_half[part, 2, h : h + 1, :rows] = jnp.sum(e * dp, axis=0, keepdims=True)

    first_pass(0, half_one)
    first_pass(1, half_two)

    def joined(stats):
        joint = jnp.maximum(stats[0][0], stats[1][0])
        weights = [jnp.exp2((stat[0] - joint) * factor) for stat in stats]
        return [joint] + [sum(stat[k] * w for stat, w in zip(stats, weights)) for k in (1, 2)]

    st_tx[0], st_tx[1], st_tx[2] = joined([st_half[0], st_half[1]])
    send(st_tx, st_rx, st_ss, st_rs, sib).wait_recv()
    joint, total, inner = joined([st_tx[...], st_rx[...]])
    inverse = 1.0 / total
    delta = inner * inverse
    for part in range(2):
        block = slice(part * mid, (part + 1) * mid)
        weight = jnp.exp2((st_half[part, 0] - joint) * factor) * inverse
        for h in range(heads):
            at = slice(h * rows, (h + 1) * rows)
            prob = e_f[block, at] * weight[h : h + 1, :rows]
            p_t[block, at] = prob.astype(BF16)
            ds_t[block, at] = (prob * (dp_f[block, at] - delta[h : h + 1, :rows])).astype(BF16)

    for side, weights, operand in ((0, ds_t, q_s), (1, p_t, g_s)):
        part_sum = jnp.dot(weights[...], operand[...], preferred_element_type=F32)
        part_sum = part_sum.reshape(2, ny, nx, part_rows, HD)
        acc[side] = part_sum[:, 0, 0]
        for ox, oy in plane:
            one_tx[oy, ox, side] = part_sum[:, oy, ox].astype(BF16)
    arriving = [
        send(one_tx.at[oy, ox], one_rx.at[oy, ox], one_ss.at[oy, ox], one_rs.at[oy, ox], in_plane(-ox, -oy))
        for ox, oy in plane
    ]
    plane_sum = acc[...]
    for copy, (ox, oy) in reversed(list(zip(arriving, plane))):
        copy.wait_recv()
        plane_sum += one_rx[oy, ox].astype(F32)
    rows_f[...] = plane_sum.reshape(2, 2 * part_rows, HD)
    for i in range(count):
        for part in range(2):
            z_tx[i, part * lanes : (part + 1) * lanes] = rows_f[part, i * lanes : (i + 1) * lanes]

    def z_copy(i):
        return pltpu.make_async_remote_copy(
            src_ref=z_tx.at[i],
            dst_ref=z_rx.at[i],
            send_sem=z_ss.at[i],
            recv_sem=z_rs.at[i],
            device_id=at_z(offsets[i]),
            device_id_type=MESH,
        )

    for i in (5, 4, 6, 1, 3, 0, 2):
        z_copy(i).start()

    @pl.when(x != 0)
    def _():
        z_copy(count - 1).start()

    @pl.when(x == 0)
    def _():
        z_rx[count - 1] = z_tx[count - 1]

    keys_t = kv[:, :, :, 0].reshape(span, HD).T
    own_cols = heads // CORES * rows
    for core in range(CORES):
        block = slice(core * own_cols, (core + 1) * own_cols)
        gq_p[core] = jnp.dot(keys_t, ds_t[:, block], preferred_element_type=F32)
    send(gq_p.at[1 - c], gq_rx, gq_ss, gq_rs, sib).wait_recv()
    gq_t = (gq_p[c] + gq_rx[...]) * scale
    for h in range(heads // CORES):
        gq_ref[0, :, h * HD : (h + 1) * HD] = gq_t[:, h * rows : (h + 1) * rows].T
    while sent:
        sent.pop().wait_send()

    for i in range(count - 1):
        z_copy(i).wait_recv()

    @pl.when(x != 0)
    def _():
        z_copy(count - 1).wait_recv()

    for h in range(KVH):
        total = jnp.zeros((2 * lanes, HD), F32)
        for i in range(count):
            source = lax.rem(z - offsets[i] + nz, nz)
            total += jnp.where(lax.div(source, half) == h, z_rx[i], 0.0)
        x_tx[h] = total
    last = [send(x_tx, x_rx.at[o], x_ss.at[o], x_rs.at[o], at_x(o)) for o in range(1, nx)]
    for i in range(count - 1):
        z_copy(i).wait_send()

    @pl.when(x != 0)
    def _():
        z_copy(count - 1).wait_send()

    for copy in last:
        copy.wait_recv()
    for h in range(KVH):
        total = x_tx[h]
        for o in range(1, nx):
            total += x_rx[o, h]
        gk_ref[:, h * HD : (h + 1) * HD] = total[:lanes] * scale
        gv_ref[:, h * HD : (h + 1) * HD] = total[lanes:]

    while sent:
        sent.pop().wait_send()


def make(mesh, ny):
    nx = mesh.shape["resp"]
    zl = mesh.shape["ep"] // ny
    zh = mesh.shape["kv"] // CORES
    geo = (nx, ny, zl, zh)
    count = zl * zh // nx

    def body(lengths, queries, grad_out, prompt_keys, prompt_values):
        rows = queries.shape[1]
        width = queries.shape[2] // mesh.shape["kv"]
        lanes = prompt_keys.shape[0]
        part_rows = count * lanes // 2
        span = 2 * nx * ny * part_rows
        both = CORES * width
        heads = both // HD
        stacked = rows * heads
        dma = pltpu.SemaphoreType.DMA
        vmem = pl.BlockSpec(memory_space=pltpu.VMEM)
        hbm = pl.BlockSpec(memory_space=pltpu.HBM)
        out_shape = (
            jax.ShapeDtypeStruct((1, rows, width), F32),
            jax.ShapeDtypeStruct(prompt_keys.shape, F32),
            jax.ShapeDtypeStruct(prompt_values.shape, F32),
        )
        operands = (lengths, queries, grad_out, prompt_keys, prompt_values)
        operands = [pltpu.with_memory_space_constraint(a, pltpu.HBM) for a in operands]
        return pl.pallas_call(
            functools.partial(kernel, geo),
            out_shape=out_shape,
            in_specs=[hbm] * 5,
            out_specs=(vmem, vmem, vmem),
            scratch_shapes=[
                pltpu.SMEM(lengths.shape, jnp.int32),
                pltpu.VMEM(prompt_keys.shape, BF16),
                pltpu.VMEM(prompt_values.shape, BF16),
                pltpu.VMEM((rows, both), BF16),
                pltpu.VMEM((rows, both), BF16),
                pltpu.VMEM((stacked, HD), BF16),
                pltpu.VMEM((stacked, HD), BF16),
                pltpu.VMEM((4 * lanes, HD), F32),
                pltpu.VMEM((4 * lanes, HD), BF16),
                pltpu.VMEM((count, 4 * lanes, HD), BF16),
                pltpu.VMEM((2, 2 * part_rows, HD), F32),
                pltpu.VMEM((2, ny, nx, 2, part_rows, HD), BF16),
                pltpu.VMEM((span, stacked), F32),
                pltpu.VMEM((span, stacked), F32),
                pltpu.VMEM((2, 3, heads, HD), F32),
                pltpu.VMEM((3, heads, HD), F32),
                pltpu.VMEM((3, heads, HD), F32),
                pltpu.VMEM((span, stacked), BF16),
                pltpu.VMEM((span, stacked), BF16),
                pltpu.VMEM((2, 2, part_rows, HD), F32),
                pltpu.VMEM((ny, nx, 2, 2, part_rows, HD), BF16),
                pltpu.VMEM((ny, nx, 2, 2, part_rows, HD), BF16),
                pltpu.VMEM((count, 2 * lanes, HD), F32),
                pltpu.VMEM((count, 2 * lanes, HD), F32),
                pltpu.VMEM((KVH, 2 * lanes, HD), F32),
                pltpu.VMEM((nx, KVH, 2 * lanes, HD), F32),
                pltpu.VMEM((CORES, HD, stacked // CORES), F32),
                pltpu.VMEM((HD, stacked // CORES), F32),
                dma((5,)),
                dma((6,)),
                dma((6,)),
                dma((2, ny, nx)),
                dma((2, ny, nx)),
                dma,
                dma,
                dma,
                dma,
                dma((ny, nx)),
                dma((ny, nx)),
                dma((count,)),
                dma((count,)),
                dma((nx,)),
                dma((nx,)),
            ],
            compiler_params=pltpu.CompilerParams(
                collective_id=0, has_side_effects=True, vmem_limit_bytes=40 * 1024 * 1024
            ),
        )(*operands)

    return jax.shard_map(
        body,
        mesh=mesh,
        in_specs=(
            P(),
            P("resp", "ep", None),
            P("resp", "ep", None),
            P(("ep", "kv"), None),
            P(("ep", "kv"), None),
        ),
        out_specs=(P("resp", "ep", "kv"), P(("ep", "kv"), None), P(("ep", "kv"), None)),
        check_vma=False,
    )


def solution(mesh):
    return make(mesh, NY)
```
